32 devices in a mesh: member: 8 (over z, x), tile: 4 (over y, core).
Axes of the slice: x: 2, y: 2, z: 4, core: 2. Of those that a mesh axis runs over, the one named last changes fastest.
Arguments:
- saturation: float32 [8, 32, 64, 128], P('member', 'tile'), may hold values from 0.05 to 0.95
- mobility: float32 [8, 32, 64, 128], P('member', 'tile'), may hold values from 0.5 to 4
- pore_scale: float32 [8, 32, 64, 128], P('member', 'tile'), may hold values from 0.5 to 1.5
- flux_x: float32 [8, 32, 64, 128], P('member', 'tile'), may hold values from -0.15 to 0.15
- flux_y: float32 [8, 32, 64, 128], P('member', 'tile'), may hold values from -0.15 to 0.15
- flux_z: float32 [8, 32, 64, 128], P('member', 'tile'), may hold values from -0.15 to 0.15
- conn_cell: int32 [1024], P('tile'), may hold values from 0 to 65535
- conn_well: int32 [1024], P('tile'), may hold values from 0 to 31
- conn_factor: float32 [1024], P('tile'), may hold values from 0.02 to 0.2
- obs_error: float32 [32, 3], P('tile'), may hold values from 0.3 to 3
Outputs:
- new_saturation: float32 [8, 32, 64, 128], P('member', 'tile')
- well_rates: float32 [8, 32, 3], P('member', 'tile')
- gram: float32 [8, 8], P('member')
The draws below stay inside these ranges and needn't reach their ends.
Inputs may be any that keep to these rules, and one draw needn't show every extreme that they name: `conn_cell`: a cell index within the block of grid rows of the tile that holds the connection, flattened over (row, layer, column). `conn_well`: a well index; any tile may hold connections of any well.
All inputs are finite; a program needn't handle non-finite values.
Results may differ from the reference program's by a relative error of at most 0.0003.
Values sent between devices are 32-bit elements; how exact they have to be, the bound alone decides.
A program may use at most 64 MiB of HBM per device.

```python
import math
import jax
import jax.numpy as jnp
import numpy as np
from jax import lax

CX = 8
NZ = 64
NY = 128
SUBSTEPS = 3
CONN_DEV = 256
NE = 8
NX = 32
NWELL = 32
CONNS = 1024


def plant(result, stream_key, least, largest):
    longest = result.shape.index(max(result.shape))
    spots = []
    for shift in (0, 1):
        where = [jax.random.randint(jax.random.fold_in(stream_key, axis), (), 0, length) for axis, length in enumerate(result.shape)]
        where[longest] = (where[longest] + shift) % result.shape[longest]
        spots.append(tuple(where))
    return result.at[spots[0]].set(least).at[spots[1]].set(largest)


def block_levels(stream_key, extent, split, least, largest):
    def one(position, shards_of):
        heights = jax.random.uniform(jax.random.fold_in(jax.random.fold_in(stream_key, 6), position), (shards_of,), jnp.float32, least / len(split), largest / len(split))
        return jnp.repeat(jnp.exp(heights), extent[position] // shards_of).reshape((-1,) + (1,) * (len(extent) - position - 1))

    level = one(*split[0])
    for cut in split[1:]:
        level = level * one(*cut)
    return level


def rank_bounds(count, skew):
    weights = [(1 << 20) // math.isqrt(standing ** skew) + 1 for standing in range(1, count + 1)]
    deviation = 1 + sum(weights) // (1 << 30)
    return np.cumsum(np.array([max(1, weight // deviation) for weight in weights]))


def skewed_ids(key, dims, number_of, skew):
    table = rank_bounds(number_of, skew)
    ticket = jax.random.randint(jax.random.fold_in(key, 1), dims, 0, int(table[number_of - 1]))
    standing = jnp.searchsorted(jnp.asarray(table, jnp.int32), ticket, side="right")
    return jax.random.permutation(jax.random.fold_in(key, 2), number_of)[standing].astype(jnp.int32)


def setup_inputs(seed: int = 0) -> dict:
    seeds = jax.random.split(jax.random.key(seed), 11)
    return {
        "saturation": jnp.clip(0.05 + 0.9 * jax.random.uniform(seeds[0], (NE, NX, NZ, NY), jnp.float32) ** block_levels(seeds[0], (NE, NX, NZ, NY), ((0, 8), (1, 4)), -0.2, 0.2), 0.05, 0.95),
        "mobility": jnp.clip(jnp.exp(math.log(4.0) - 2.0794415 * jax.random.uniform(seeds[1], (NE, NX, NZ, NY), jnp.float32) ** block_levels(seeds[1], (NE, NX, NZ, NY), ((0, 8), (1, 4)), -0.2, 0.2)), 0.5, 4.0),
        "pore_scale": jnp.clip(jnp.exp(math.log(1.5) - 1.0986123 * jax.random.uniform(seeds[2], (NE, NX, NZ, NY), jnp.float32) ** block_levels(seeds[2], (NE, NX, NZ, NY), ((0, 8), (1, 4)), -0.2, 0.2)), 0.5, 1.5),
        "flux_x": jnp.clip(jax.random.uniform(seeds[3], (NE, NX, NZ, NY), jnp.float32, -0.15, 0.15) * block_levels(seeds[3], (NE, NX, NZ, NY), ((0, 8), (1, 4)), -0.4, 0.0), -0.15, 0.15),
        "flux_y": jnp.clip(jax.random.uniform(seeds[4], (NE, NX, NZ, NY), jnp.float32, -0.15, 0.15) * block_levels(seeds[4], (NE, NX, NZ, NY), ((0, 8), (1, 4)), -0.4, 0.0), -0.15, 0.15),
        "flux_z": jnp.clip(jax.random.uniform(seeds[5], (NE, NX, NZ, NY), jnp.float32, -0.15, 0.15) * block_levels(seeds[5], (NE, NX, NZ, NY), ((0, 8), (1, 4)), -0.4, 0.0), -0.15, 0.15),
        "conn_cell": plant(jax.random.randint(seeds[6], (CONNS,), 0, CX * NZ * NY), jax.random.fold_in(seeds[6], 1), 0, (CX * NZ * NY) - 1).astype(jnp.int32),
        "conn_well": plant(skewed_ids(seeds[7], (CONNS,), NWELL, 2), jax.random.fold_in(seeds[7], 3), 0, NWELL - 1).astype(jnp.int32),
        "conn_factor": jnp.clip(jnp.exp(math.log(0.2) - 2.3025851 * jax.random.uniform(seeds[8], (CONNS,), jnp.float32) ** block_levels(seeds[8], (CONNS,), ((0, 4),), -0.2, 0.2)), 0.02, 0.2),
        "obs_error": jnp.clip(jnp.exp(math.log(3.0) - 2.3025851 * jax.random.uniform(seeds[9], (NWELL, SUBSTEPS), jnp.float32) ** block_levels(seeds[9], (NWELL, SUBSTEPS), ((0, 4),), -0.2, 0.2)), 0.3, 3.0),
    }


def frac(sat, mob):
    wet = sat * sat
    dry = (1.0 - sat) * (1.0 - sat)
    return wet / (wet + mob * dry)


def lower(field, axis):
    count = field.shape[axis]
    zero = jnp.zeros_like(lax.slice_in_dim(field, 0, 1, axis=axis))
    return jnp.concatenate([zero, lax.slice_in_dim(field, 0, count - 1, axis=axis)], axis=axis)


def upper(field, axis):
    count = field.shape[axis]
    zero = jnp.zeros_like(lax.slice_in_dim(field, 0, 1, axis=axis))
    return jnp.concatenate([lax.slice_in_dim(field, 1, count, axis=axis), zero], axis=axis)


def divergence(flow, flux, axis):
    face = jnp.maximum(flux, 0.0) * lower(flow, axis) + jnp.minimum(flux, 0.0) * flow
    return upper(face, axis) - face


def masked(flux, axis):
    place = lax.broadcasted_iota(jnp.int32, flux.shape, axis)
    return jnp.where(place > 0, flux, jnp.zeros_like(flux))


def reference(saturation, mobility, pore_scale, flux_x, flux_y, flux_z, conn_cell, conn_well, conn_factor, obs_error):
    members = saturation.shape[0]
    tile_of = (jnp.arange(CONNS, dtype=jnp.int32) // CONN_DEV).astype(jnp.int32)
    cells = (tile_of * (CX * NZ * NY) + conn_cell).astype(jnp.int32)

    def member_run(items):
        sat, mob, pore, qx, qy, qz = items
        qx = masked(qx, 0)
        qz = masked(qz, 1)
        qy = masked(qy, 2)
        mob_flat = mob.reshape(-1)[cells]
        parts = []
        for step in range(SUBSTEPS):
            flow = frac(sat, mob)
            total = divergence(flow, qx, 0) + divergence(flow, qz, 1) + divergence(flow, qy, 2)
            sat = sat - pore * total
            parts.append(conn_factor * frac(sat.reshape(-1)[cells], mob_flat))
        return sat, jnp.stack(parts, -1)

    new_saturation, contrib = lax.map(member_run, (saturation, mobility, pore_scale, flux_x, flux_y, flux_z))
    rates = jax.ops.segment_sum(jnp.transpose(contrib, (1, 0, 2)), conn_well, num_segments=NWELL)
    well_rates = jnp.transpose(rates, (1, 0, 2))
    data = (well_rates / obs_error[None]).reshape(members, -1)
    centered = data - jnp.mean(data, axis=0, keepdims=True)
    gram = jnp.dot(centered, centered.T, precision=lax.Precision.HIGHEST) / (members - 1.0)
    return new_saturation, well_rates, gram
```

```python
import functools

import jax
import jax.numpy as jnp
from jax import lax
from jax.experimental import pallas as pl
from jax.experimental.pallas import tpu as pltpu
from jax.sharding import PartitionSpec as P

SUBSTEPS = 3
LANES = 128
SUBLANES = 8
MESH = pl.DeviceIdType.MESH


def frac(sat, mob):
    wet = sat * sat
    rest = 1.0 - sat
    return wet / (wet + mob * (rest * rest))


def face(flux, below, here):
    return jnp.maximum(flux, 0.0) * below + jnp.minimum(flux, 0.0) * here


def columns_of(row):
    return jnp.transpose(jnp.broadcast_to(row, (LANES, row.shape[1])))


def kernel(
    tiles,
    members,
    sat_hbm,
    mob_hbm,
    pore_hbm,
    qx_hbm,
    qy_hbm,
    qz_hbm,
    cell_hbm,
    well_hbm,
    factor_hbm,
    obs_hbm,
    new_ref,
    rates_ref,
    gram_ref,
    sat,
    mob,
    pore,
    qx,
    qy,
    qz,
    cell_ref,
    well_ref,
    factor_ref,
    obs_ref,
    flow,
    halo_lo,
    halo_hi,
    q_above,
    split,
    pick,
    lane_mask,
    well_mask,
    obs_all,
    sums,
    data,
    in_sem,
    halo_send,
    halo_recv,
    q_send,
    q_recv,
    obs_send,
    obs_recv,
    sum_send,
    sum_recv,
    data_send,
    data_recv,
):
    tile = lax.axis_index("tile")
    member = lax.axis_index("member")
    rows, layers, columns = sat.shape
    last = rows - 1
    wells_dev = obs_ref.shape[1]
    conns = cell_ref.shape[1]
    has_lo = tile > 0
    has_hi = tile < tiles - 1

    loads = [
        pltpu.make_async_copy(src, dst, in_sem.at[n])
        for n, (src, dst) in enumerate(
            (
                (sat_hbm.at[0], sat),
                (mob_hbm.at[0], mob),
                (qx_hbm.at[0], qx),
                (qz_hbm.at[0], qz),
                (qy_hbm.at[0], qy),
                (pore_hbm.at[0], pore),
                (obs_hbm, obs_ref),
                (cell_hbm, cell_ref),
                (well_hbm, well_ref),
                (factor_hbm, factor_ref),
            )
        )
    ]
    for load in loads:
        load.start()

    barrier = pltpu.get_barrier_semaphore()
    for d in range(1, tiles):
        pl.semaphore_signal(
            barrier, inc=1, device_id={"tile": lax.rem(tile + d, tiles)}, device_id_type=MESH
        )
    for d in range(1, members):
        pl.semaphore_signal(
            barrier, inc=1, device_id={"member": lax.rem(member + d, members)}, device_id_type=MESH
        )

    pl.semaphore_wait(barrier, tiles + members - 2)

    def exchange(src, dst_at, peers, axis, me, send_sem, recv_sem):
        copies = []
        for d in range(1, peers):
            copies.append(
                pltpu.make_async_remote_copy(
                    src_ref=src,
                    dst_ref=dst_at,
                    send_sem=send_sem.at[d - 1],
                    recv_sem=recv_sem.at[d - 1],
                    device_id={axis: lax.rem(me + d, peers)},
                    device_id_type=MESH,
                )
            )
            copies[-1].start()
        return copies

    q_copy = pltpu.make_async_remote_copy(
        src_ref=qx_hbm.at[0, 0],
        dst_ref=q_above,
        send_sem=q_send,
        recv_sem=q_recv,
        device_id={"tile": jnp.maximum(tile - 1, 0)},
        device_id_type=MESH,
    )

    def halo_copies(k):
        down = pltpu.make_async_remote_copy(
            src_ref=flow.at[k, 0],
            dst_ref=halo_hi.at[k],
            send_sem=halo_send.at[k, 0],
            recv_sem=halo_recv.at[k, 0],
            device_id={"tile": jnp.maximum(tile - 1, 0)},
            device_id_type=MESH,
        )
        up = pltpu.make_async_remote_copy(
            src_ref=flow.at[k, last],
            dst_ref=halo_lo.at[k],
            send_sem=halo_send.at[k, 1],
            recv_sem=halo_recv.at[k, 1],
            device_id={"tile": jnp.minimum(tile + 1, tiles - 1)},
            device_id_type=MESH,
        )
        return down, up

    halos = [halo_copies(k) for k in range(SUBSTEPS)]

    def send_halo(k):
        down, up = halos[k]

        @pl.when(has_lo)
        def _():
            down.start()

        @pl.when(has_hi)
        def _():
            up.start()

    def set_flow(k, i, value):
        flow[k, i] = value

    def set_split(i, value):
        high = value.astype(jnp.bfloat16)
        at = pl.ds(pl.multiple_of(i * layers, layers), layers)
        split[at, 0:columns] = high
        split[at, columns : 2 * columns] = (value - high.astype(jnp.float32)).astype(jnp.bfloat16)

    loads[0].wait()
    loads[1].wait()
    set_flow(0, 0, frac(sat[0], mob[0]))
    set_flow(0, last, frac(sat[last], mob[last]))
    send_halo(0)

    @pl.when(has_lo)
    def _():
        q_copy.start()

    loads[6].wait()
    obs_all[tile] = jnp.ones((SUBLANES, LANES), jnp.float32)
    obs_all[tile, 0:SUBSTEPS, 0:wells_dev] = obs_ref[...]
    obs_copies = exchange(obs_all.at[tile], obs_all.at[tile], tiles, "tile", tile, obs_send, obs_recv)

    def first_flow(i, carry):
        set_flow(0, i, frac(sat[i], mob[i]))
        return carry

    lax.fori_loop(1, last, first_flow, 0, unroll=True)
    for load in loads[2:6]:
        load.wait()

    col_ids = lax.broadcasted_iota(jnp.int32, (layers, columns), 1)
    lay_ids = lax.broadcasted_iota(jnp.int32, (layers, columns), 0)

    def update(k, i, face_lo, face_hi):
        here = flow[k, i]
        qz_i = jnp.where(lay_ids > 0, qz[i], 0.0)
        qy_i = jnp.where(col_ids > 0, qy[i], 0.0)
        face_z = face(qz_i, pltpu.roll(here, 1, 0), here)
        face_y = face(qy_i, pltpu.roll(here, 1, 1), here)
        total = face_hi - face_lo
        total = total + (pltpu.roll(face_z, layers - 1, 0) - face_z)
        total = total + (pltpu.roll(face_y, columns - 1, 1) - face_y)
        after = sat[i] - pore[i] * total
        if k + 1 < SUBSTEPS:
            sat[i] = after
        else:
            new_ref[0, i] = after
        value = frac(after, mob[i])
        set_flow(k + 1, i, value)
        set_split(i, value)

    def set_masks():
        for load in loads[7:]:
            load.wait()
        lane_ids = lax.broadcasted_iota(jnp.int32, (conns, LANES), 1)
        cell_col = columns_of(cell_ref[...])
        row_col = lax.shift_right_logical(cell_col, columns.bit_length() - 1)
        for b in range(rows * layers // LANES):
            pick[:, b * LANES : (b + 1) * LANES] = jnp.where(
                row_col == lane_ids + b * LANES, 1.0, 0.0
            ).astype(jnp.bfloat16)
        lane_mask[...] = jnp.where(
            cell_col - row_col * columns == lane_ids, columns_of(factor_ref[...]), 0.0
        )
        well_mask[...] = jnp.where(columns_of(well_ref[...]) == lane_ids, 1.0, 0.0)

    step_rates = []
    for k in range(SUBSTEPS):
        def inner(i, face_lo, k=k):
            face_hi = face(qx[i + 1], flow[k, i], flow[k, i + 1])
            update(k, i, face_lo, face_hi)
            return face_hi

        face_one = face(qx[1], flow[k, 0], flow[k, 1])
        face_last = lax.fori_loop(1, last, inner, face_one, unroll=True)
        if k == 0:
            set_masks()

        down, up = halos[k]

        @pl.when(has_lo)
        def _():
            up.wait_recv()

        @pl.when(has_hi)
        def _():
            down.wait_recv()

        if k == 0:

            @pl.when(has_hi)
            def _():
                q_copy.wait_recv()

            @pl.when(jnp.logical_not(has_hi))
            def _():
                q_above[...] = jnp.zeros_like(q_above)

        below = jnp.where(has_lo, halo_lo[k], 0.0)
        above = jnp.where(has_hi, halo_hi[k], 0.0)
        qx_first = jnp.where(has_lo, qx[0], 0.0)
        update(k, 0, face(qx_first, below, flow[k, 0]), face_one)
        update(k, last, face_last, face(q_above[...], flow[k, last], above))
        if k + 1 < SUBSTEPS:
            send_halo(k + 1)
        found = jnp.dot(pick[...], split[...], preferred_element_type=jnp.float32)
        found = (found[:, 0:columns] + found[:, columns : 2 * columns]) * lane_mask[...]
        rate = jnp.sum(found, axis=1, keepdims=True) * well_mask[...]
        step_rates.append(jnp.sum(rate, axis=0, keepdims=True))

    step_rates.append(jnp.zeros((SUBLANES - SUBSTEPS, LANES), jnp.float32))
    sums[tile] = jnp.concatenate(step_rates, axis=0)
    sum_copies = exchange(sums.at[tile], sums.at[tile], tiles, "tile", tile, sum_send, sum_recv)
    for copy in obs_copies:
        copy.wait_recv()
    lane_row = lax.broadcasted_iota(jnp.int32, (SUBLANES, LANES), 1)
    obs_whole = obs_all[0]
    for t in range(1, tiles):
        moved = pltpu.roll(obs_all[t], t * wells_dev, 1)
        obs_whole = jnp.where(lane_row >= t * wells_dev, moved, obs_whole)
    for copy in sum_copies:
        copy.wait_recv()
    whole = sums[0]
    for t in range(1, tiles):
        whole = whole + sums[t]
    data[member] = whole / obs_whole
    data_copies = exchange(
        data.at[member], data.at[member], members, "member", member, data_send, data_recv
    )
    mine = pltpu.roll(whole, lax.rem(LANES - tile * wells_dev, LANES), 1)
    for k in range(SUBSTEPS):
        rates_ref[k] = mine[k : k + 1, 0:wells_dev]

    for copy in data_copies:
        copy.wait_recv()
    mean = data[0]
    for m in range(1, members):
        mean = mean + data[m]
    mean = mean * (1.0 / members)
    own = data[member] - mean
    terms = jnp.concatenate(
        [jnp.sum(own * (data[m] - mean), axis=0, keepdims=True) for m in range(members)], axis=0
    )
    terms = jnp.sum(terms, axis=1, keepdims=True)
    square = (members, LANES)
    diagonal = lax.broadcasted_iota(jnp.int32, square, 0) == lax.broadcasted_iota(
        jnp.int32, square, 1
    )
    line = jnp.sum(jnp.where(diagonal, terms, 0.0), axis=0, keepdims=True)
    gram_ref[...] = line[:, 0:members] / (members - 1.0)

    for down, up in halos:

        @pl.when(has_lo)
        def _():
            down.wait_send()

        @pl.when(has_hi)
        def _():
            up.wait_send()

    @pl.when(has_lo)
    def _():
        q_copy.wait_send()

    for copy in obs_copies + sum_copies + data_copies:
        copy.wait_send()


def body(tiles, members, sat, mob, pore, qx, qy, qz, cell, well, factor, obs):
    block = sat.shape[1:]
    rows, layers, columns = block
    conns = cell.shape[0]
    wells_dev = obs.shape[0]
    f32 = jnp.float32
    dma = pltpu.SemaphoreType.DMA
    hbm_spec = pl.BlockSpec(memory_space=pltpu.HBM)
    vmem_spec = pl.BlockSpec(memory_space=pltpu.VMEM)
    new, rates, gram = pl.pallas_call(
        functools.partial(kernel, tiles, members),
        out_shape=(
            jax.ShapeDtypeStruct(sat.shape, f32),
            jax.ShapeDtypeStruct((SUBSTEPS, 1, wells_dev), f32),
            jax.ShapeDtypeStruct((1, members), f32),
        ),
        in_specs=[hbm_spec] * 10,
        out_specs=(vmem_spec,) * 3,
        scratch_shapes=[pltpu.VMEM(block, f32)] * 6
        + [
            pltpu.VMEM((1, conns), jnp.int32),
            pltpu.VMEM((1, conns), jnp.int32),
            pltpu.VMEM((1, conns), f32),
            pltpu.VMEM((SUBSTEPS, wells_dev), f32),
            pltpu.VMEM((SUBSTEPS + 1,) + block, f32),
            pltpu.VMEM((SUBSTEPS, layers, columns), f32),
            pltpu.VMEM((SUBSTEPS, layers, columns), f32),
            pltpu.VMEM((layers, columns), f32),
            pltpu.VMEM((rows * layers, 2 * columns), jnp.bfloat16),
            pltpu.VMEM((conns, rows * layers), jnp.bfloat16),
            pltpu.VMEM((conns, LANES), f32),
            pltpu.VMEM((conns, LANES), f32),
            pltpu.VMEM((tiles, SUBLANES, LANES), f32),
            pltpu.VMEM((tiles, SUBLANES, LANES), f32),
            pltpu.VMEM((members, SUBLANES, LANES), f32),
            dma((10,)),
            dma((SUBSTEPS, 2)),
            dma((SUBSTEPS, 2)),
            dma(()),
            dma(()),
            dma((tiles - 1,)),
            dma((tiles - 1,)),
            dma((tiles - 1,)),
            dma((tiles - 1,)),
            dma((members - 1,)),
            dma((members - 1,)),
        ],
        compiler_params=pltpu.CompilerParams(
            collective_id=0, has_side_effects=True, vmem_limit_bytes=60 * 1024 * 1024
        ),
        cost_estimate=pl.CostEstimate(
            flops=100 * SUBSTEPS * rows * layers * columns,
            bytes_accessed=28 * rows * layers * columns,
            transcendentals=0,
        ),
        name="transport",
    )(sat, mob, pore, qx, qy, qz, cell.reshape(1, -1), well.reshape(1, -1), factor.reshape(1, -1), obs.T)
    return new, jnp.transpose(rates, (1, 2, 0)), gram


def solution(mesh):
    field = P("member", "tile", None, None)
    in_specs = (field,) * 6 + (P("tile"), P("tile"), P("tile"), P("tile", None))
    out_specs = (field, P("member", "tile", None), P("member", None))
    run = functools.partial(body, mesh.shape["tile"], mesh.shape["member"])
    return jax.shard_map(run, mesh=mesh, in_specs=in_specs, out_specs=out_specs, check_vma=False)
```

```python
import functools

import jax
import jax.numpy as jnp
from jax import lax
from jax.experimental import pallas as pl
from jax.experimental.pallas import tpu as pltpu
from jax.sharding import PartitionSpec as P

SUBSTEPS = 3
LANES = 128
SUBLANES = 8
MESH = pl.DeviceIdType.MESH
RUN_VMEM = 60 * 1024 * 1024
OUT_VMEM = 4 * 1024 * 1024


def frac(sat, mob):
    wet = sat * sat
    rest = 1.0 - sat
    return wet / (wet + mob * (rest * rest))


def face(flux, below, here):
    return jnp.maximum(flux, 0.0) * below + jnp.minimum(flux, 0.0) * here


def columns_of(row):
    return jnp.transpose(jnp.broadcast_to(row, (LANES, row.shape[1])))


def kernel(
    tiles,
    members,
    sat_hbm,
    mob_hbm,
    pore_hbm,
    qx_hbm,
    qy_hbm,
    qz_hbm,
    cell_hbm,
    well_hbm,
    factor_hbm,
    obs_hbm,
    new_ref,
    whole_ref,
    data,
    sat,
    mob,
    pore,
    qx,
    qy,
    qz,
    cell_ref,
    well_ref,
    factor_ref,
    obs_ref,
    flow,
    halo_lo,
    halo_hi,
    q_above,
    split,
    pick,
    lane_mask,
    well_mask,
    obs_all,
    sums,
    in_sem,
    halo_send,
    halo_recv,
    q_send,
    q_recv,
    obs_send,
    obs_recv,
    sum_send,
    sum_recv,
    data_send,
    data_recv,
):
    tile = lax.axis_index("tile")
    member = lax.axis_index("member")
    rows, layers, columns = sat.shape
    last = rows - 1
    wells_dev = obs_ref.shape[1]
    conns = cell_ref.shape[1]
    has_lo = tile > 0
    has_hi = tile < tiles - 1

    loads = [
        pltpu.make_async_copy(src, dst, in_sem.at[n])
        for n, (src, dst) in enumerate(
            (
                (sat_hbm.at[0, 0], sat.at[0]),
                (mob_hbm.at[0, 0], mob.at[0]),
                (sat_hbm.at[0, last], sat.at[last]),
                (mob_hbm.at[0, last], mob.at[last]),
                (sat_hbm.at[0, 1:last], sat.at[1:last]),
                (mob_hbm.at[0, 1:last], mob.at[1:last]),
                (qx_hbm.at[0], qx),
                (qz_hbm.at[0], qz),
                (qy_hbm.at[0], qy),
                (pore_hbm.at[0], pore),
                (obs_hbm, obs_ref),
                (cell_hbm, cell_ref),
                (well_hbm, well_ref),
                (factor_hbm, factor_ref),
            )
        )
    ]
    for load in loads:
        load.start()

    barrier = pltpu.get_barrier_semaphore()
    for d in range(1, tiles):
        pl.semaphore_signal(
            barrier, inc=1, device_id={"tile": lax.rem(tile + d, tiles)}, device_id_type=MESH
        )
    for d in range(1, members):
        pl.semaphore_signal(
            barrier, inc=1, device_id={"member": lax.rem(member + d, members)}, device_id_type=MESH
        )

    pl.semaphore_wait(barrier, tiles + members - 2)

    def exchange(src, dst_at, peers, axis, me, send_sem, recv_sem):
        copies = []
        for d in range(1, peers):
            copies.append(
                pltpu.make_async_remote_copy(
                    src_ref=src,
                    dst_ref=dst_at,
                    send_sem=send_sem.at[d - 1],
                    recv_sem=recv_sem.at[d - 1],
                    device_id={axis: lax.rem(me + d, peers)},
                    device_id_type=MESH,
                )
            )
            copies[-1].start()
        return copies

    q_copy = pltpu.make_async_remote_copy(
        src_ref=qx_hbm.at[0, 0],
        dst_ref=q_above,
        send_sem=q_send,
        recv_sem=q_recv,
        device_id={"tile": jnp.maximum(tile - 1, 0)},
        device_id_type=MESH,
    )

    def halo_copies(k):
        down = pltpu.make_async_remote_copy(
            src_ref=flow.at[k, 0],
            dst_ref=halo_hi.at[k],
            send_sem=halo_send.at[k, 0],
            recv_sem=halo_recv.at[k, 0],
            device_id={"tile": jnp.maximum(tile - 1, 0)},
            device_id_type=MESH,
        )
        up = pltpu.make_async_remote_copy(
            src_ref=flow.at[k, last],
            dst_ref=halo_lo.at[k],
            send_sem=halo_send.at[k, 1],
            recv_sem=halo_recv.at[k, 1],
            device_id={"tile": jnp.minimum(tile + 1, tiles - 1)},
            device_id_type=MESH,
        )
        return down, up

    halos = [halo_copies(k) for k in range(SUBSTEPS)]

    def send_halo(k):
        down, up = halos[k]

        @pl.when(has_lo)
        def _():
            down.start()

        @pl.when(has_hi)
        def _():
            up.start()

    def set_flow(k, i, value):
        flow[k, i] = value

    def set_split(i, value):
        high = value.astype(jnp.bfloat16)
        place = {0: 0, last: 1}[i] if isinstance(i, int) else i + 1
        at = pl.ds(pl.multiple_of(place * layers, layers), layers)
        split[at, 0:columns] = high
        split[at, columns : 2 * columns] = (value - high.astype(jnp.float32)).astype(jnp.bfloat16)

    for load in loads[0:4]:
        load.wait()
    set_flow(0, 0, frac(sat[0], mob[0]))
    set_flow(0, last, frac(sat[last], mob[last]))
    send_halo(0)

    @pl.when(has_lo)
    def _():
        q_copy.start()

    loads[10].wait()
    obs_all[tile] = jnp.ones((SUBLANES, LANES), jnp.float32)
    obs_all[tile, 0:SUBSTEPS, 0:wells_dev] = obs_ref[...]
    obs_copies = exchange(obs_all.at[tile], obs_all.at[tile], tiles, "tile", tile, obs_send, obs_recv)

    def first_flow(i, carry):
        set_flow(0, i, frac(sat[i], mob[i]))
        return carry

    for load in loads[4:6]:
        load.wait()
    lax.fori_loop(1, last, first_flow, 0, unroll=True)
    for load in loads[6:10]:
        load.wait()

    col_ids = lax.broadcasted_iota(jnp.int32, (layers, columns), 1)
    lay_ids = lax.broadcasted_iota(jnp.int32, (layers, columns), 0)

    def update(k, i, face_lo, face_hi):
        here = flow[k, i]
        qz_i = jnp.where(lay_ids > 0, qz[i], 0.0)
        qy_i = jnp.where(col_ids > 0, qy[i], 0.0)
        face_z = face(qz_i, pltpu.roll(here, 1, 0), here)
        face_y = face(qy_i, pltpu.roll(here, 1, 1), here)
        total = face_hi - face_lo
        total = total + (pltpu.roll(face_z, layers - 1, 0) - face_z)
        total = total + (pltpu.roll(face_y, columns - 1, 1) - face_y)
        after = sat[i] - pore[i] * total
        if k + 1 < SUBSTEPS:
            sat[i] = after
        else:
            new_ref[0, i] = after
        value = frac(after, mob[i])
        set_flow(k + 1, i, value)
        set_split(i, value)

    def set_masks():
        for load in loads[11:]:
            load.wait()
        lane_ids = lax.broadcasted_iota(jnp.int32, (conns, LANES), 1)
        cell_col = columns_of(cell_ref[...])
        row_col = lax.shift_right_logical(cell_col, columns.bit_length() - 1)
        spot = jnp.where(row_col < layers, row_col, row_col + layers)
        spot = jnp.where(row_col < last * layers, spot, row_col - (last - 1) * layers)
        for b in range(rows * layers // LANES):
            pick[:, b * LANES : (b + 1) * LANES] = jnp.where(
                spot == lane_ids + b * LANES, 1.0, 0.0
            ).astype(jnp.bfloat16)
        lane_mask[...] = jnp.where(
            cell_col - row_col * columns == lane_ids, columns_of(factor_ref[...]), 0.0
        )
        well_mask[...] = jnp.where(columns_of(well_ref[...]) == lane_ids, 1.0, 0.0)

    step_rates = []
    edge = 2 * layers

    def gather(start, stop):
        found = jnp.dot(
            pick[:, start:stop], split[start:stop, :], preferred_element_type=jnp.float32
        )
        return found[:, 0:columns] + found[:, columns : 2 * columns]

    def add_rates(found):
        rate = jnp.sum(found * lane_mask[...], axis=1, keepdims=True) * well_mask[...]
        step_rates.append(jnp.sum(rate, axis=0, keepdims=True))

    for k in range(SUBSTEPS):
        if k > 0:
            add_rates(gather(0, rows * layers))

        def inner(i, face_lo, k=k):
            face_hi = face(qx[i + 1], flow[k, i], flow[k, i + 1])
            update(k, i, face_lo, face_hi)
            return face_hi

        face_one = face(qx[1], flow[k, 0], flow[k, 1])
        face_last = lax.fori_loop(1, last, inner, face_one, unroll=True)
        if k == 0:
            set_masks()
        if k + 1 == SUBSTEPS:
            found_inner = gather(edge, rows * layers)

        down, up = halos[k]

        @pl.when(has_lo)
        def _():
            up.wait_recv()

        @pl.when(has_hi)
        def _():
            down.wait_recv()

        if k == 0:

            @pl.when(has_hi)
            def _():
                q_copy.wait_recv()

            @pl.when(jnp.logical_not(has_hi))
            def _():
                q_above[...] = jnp.zeros_like(q_above)

        below = jnp.where(has_lo, halo_lo[k], 0.0)
        above = jnp.where(has_hi, halo_hi[k], 0.0)
        qx_first = jnp.where(has_lo, qx[0], 0.0)
        update(k, 0, face(qx_first, below, flow[k, 0]), face_one)
        update(k, last, face_last, face(q_above[...], flow[k, last], above))
        if k + 1 < SUBSTEPS:
            send_halo(k + 1)
    add_rates(found_inner + gather(0, edge))
    step_rates.append(jnp.zeros((SUBLANES - SUBSTEPS, LANES), jnp.float32))
    sums[tile] = jnp.concatenate(step_rates, axis=0)
    sum_copies = exchange(sums.at[tile], sums.at[tile], tiles, "tile", tile, sum_send, sum_recv)
    for copy in obs_copies:
        copy.wait_recv()
    lane_row = lax.broadcasted_iota(jnp.int32, (SUBLANES, LANES), 1)
    obs_whole = obs_all[0]
    for t in range(1, tiles):
        moved = pltpu.roll(obs_all[t], t * wells_dev, 1)
        obs_whole = jnp.where(lane_row >= t * wells_dev, moved, obs_whole)
    for copy in sum_copies:
        copy.wait_recv()
    whole = sums[0]
    for t in range(1, tiles):
        whole = whole + sums[t]
    data[member] = whole / obs_whole
    data_copies = exchange(
        data.at[member], data.at[member], members, "member", member, data_send, data_recv
    )
    whole_ref[...] = whole
    for copy in data_copies:
        copy.wait_recv()

    for down, up in halos:

        @pl.when(has_lo)
        def _():
            down.wait_send()

        @pl.when(has_hi)
        def _():
            up.wait_send()

    @pl.when(has_lo)
    def _():
        q_copy.wait_send()

    for copy in obs_copies + sum_copies + data_copies:
        copy.wait_send()


def finish(new_ref, whole_ref, data, new_hbm, rates_hbm, gram_hbm, rates, gram, out_sem):
    tile = lax.axis_index("tile")
    member = lax.axis_index("member")
    members = data.shape[0]
    wells_dev = rates.shape[2]
    new_out = pltpu.make_async_copy(new_ref, new_hbm, out_sem.at[0])
    new_out.start()
    mine = pltpu.roll(whole_ref[...], lax.rem(LANES - tile * wells_dev, LANES), 1)
    for k in range(SUBSTEPS):
        rates[k] = mine[k : k + 1, 0:wells_dev]
    rates_out = pltpu.make_async_copy(rates, rates_hbm, out_sem.at[1])
    rates_out.start()
    mean = data[0]
    for m in range(1, members):
        mean = mean + data[m]
    mean = mean * (1.0 / members)
    own = data[member] - mean
    terms = jnp.concatenate(
        [jnp.sum(own * (data[m] - mean), axis=0, keepdims=True) for m in range(members)], axis=0
    )
    terms = jnp.sum(terms, axis=1, keepdims=True)
    square = (members, LANES)
    diagonal = lax.broadcasted_iota(jnp.int32, square, 0) == lax.broadcasted_iota(
        jnp.int32, square, 1
    )
    line = jnp.sum(jnp.where(diagonal, terms, 0.0), axis=0, keepdims=True)
    gram[...] = line[:, 0:members] / (members - 1.0)
    gram_out = pltpu.make_async_copy(gram, gram_hbm, out_sem.at[2])
    gram_out.start()
    new_out.wait()
    rates_out.wait()
    gram_out.wait()


def body(tiles, members, sat, mob, pore, qx, qy, qz, cell, well, factor, obs):
    block = sat.shape[1:]
    rows, layers, columns = block
    conns = cell.shape[0]
    wells_dev = obs.shape[0]
    f32 = jnp.float32
    dma = pltpu.SemaphoreType.DMA
    hbm_spec = pl.BlockSpec(memory_space=pltpu.HBM)
    vmem_spec = pl.BlockSpec(memory_space=pltpu.VMEM)
    new, whole, data = pl.pallas_call(
        functools.partial(kernel, tiles, members),
        out_shape=(
            pltpu.VMEM(sat.shape, f32),
            pltpu.VMEM((SUBLANES, LANES), f32),
            pltpu.VMEM((members, SUBLANES, LANES), f32),
        ),
        in_specs=[hbm_spec] * 10,
        out_specs=(vmem_spec,) * 3,
        scratch_shapes=[pltpu.VMEM(block, f32)] * 6
        + [
            pltpu.VMEM((1, conns), jnp.int32),
            pltpu.VMEM((1, conns), jnp.int32),
            pltpu.VMEM((1, conns), f32),
            pltpu.VMEM((SUBSTEPS, wells_dev), f32),
            pltpu.VMEM((SUBSTEPS + 1,) + block, f32),
            pltpu.VMEM((SUBSTEPS, layers, columns), f32),
            pltpu.VMEM((SUBSTEPS, layers, columns), f32),
            pltpu.VMEM((layers, columns), f32),
            pltpu.VMEM((rows * layers, 2 * columns), jnp.bfloat16),
            pltpu.VMEM((conns, rows * layers), jnp.bfloat16),
            pltpu.VMEM((conns, LANES), f32),
            pltpu.VMEM((conns, LANES), f32),
            pltpu.VMEM((tiles, SUBLANES, LANES), f32),
            pltpu.VMEM((tiles, SUBLANES, LANES), f32),
            dma((14,)),
            dma((SUBSTEPS, 2)),
            dma((SUBSTEPS, 2)),
            dma(()),
            dma(()),
            dma((tiles - 1,)),
            dma((tiles - 1,)),
            dma((tiles - 1,)),
            dma((tiles - 1,)),
            dma((members - 1,)),
            dma((members - 1,)),
        ],
        compiler_params=pltpu.CompilerParams(
            collective_id=0, has_side_effects=True, vmem_limit_bytes=RUN_VMEM
        ),
        cost_estimate=pl.CostEstimate(
            flops=100 * SUBSTEPS * rows * layers * columns,
            bytes_accessed=28 * rows * layers * columns,
            transcendentals=0,
        ),
        name="transport",
    )(sat, mob, pore, qx, qy, qz, cell.reshape(1, -1), well.reshape(1, -1), factor.reshape(1, -1), obs.T)
    new, rates, gram = pl.pallas_call(
        finish,
        out_shape=(
            jax.ShapeDtypeStruct(sat.shape, f32),
            jax.ShapeDtypeStruct((SUBSTEPS, 1, wells_dev), f32),
            jax.ShapeDtypeStruct((1, members), f32),
        ),
        in_specs=[vmem_spec] * 3,
        out_specs=(hbm_spec,) * 3,
        scratch_shapes=[
            pltpu.VMEM((SUBSTEPS, 1, wells_dev), f32),
            pltpu.VMEM((1, members), f32),
            dma((3,)),
        ],
        compiler_params=pltpu.CompilerParams(vmem_limit_bytes=OUT_VMEM),
        name="finish",
    )(new, whole, data)
    return new, jnp.transpose(rates, (1, 2, 0)), gram


def solution(mesh):
    field = P("member", "tile", None, None)
    in_specs = (field,) * 6 + (P("tile"), P("tile"), P("tile"), P("tile", None))
    out_specs = (field, P("member", "tile", None), P("member", None))
    run = functools.partial(body, mesh.shape["tile"], mesh.shape["member"])
    return jax.shard_map(run, mesh=mesh, in_specs=in_specs, out_specs=out_specs, check_vma=False)
```

```python
import functools

import jax
import jax.numpy as jnp
from jax import lax
from jax.experimental import pallas as pl
from jax.experimental.pallas import tpu as pltpu
from jax.sharding import PartitionSpec as P

SUBSTEPS = 3
LANES = 128
SUBLANES = 8
MESH = pl.DeviceIdType.MESH
RUN_VMEM = 60 * 1024 * 1024
OUT_VMEM = 4 * 1024 * 1024


def frac(sat, mob):
    wet = sat * sat
    rest = 1.0 - sat
    whole = wet + mob * (rest * rest)
    inverse = pl.reciprocal(whole, approx=True)
    return wet * (inverse * (2.0 - whole * inverse))


def face(flux, below, here):
    return jnp.maximum(flux, 0.0) * below + jnp.minimum(flux, 0.0) * here


def columns_of(row):
    return jnp.transpose(jnp.broadcast_to(row, (LANES, row.shape[1])))


def kernel(
    tiles,
    members,
    sat_hbm,
    mob_hbm,
    pore_hbm,
    qx_hbm,
    qy_hbm,
    qz_hbm,
    cell_hbm,
    well_hbm,
    factor_hbm,
    obs_hbm,
    new_ref,
    whole_ref,
    data,
    sat,
    mob,
    pore,
    qx,
    qy,
    qz,
    cell_ref,
    well_ref,
    factor_ref,
    obs_ref,
    flow,
    halo_lo,
    halo_hi,
    q_above,
    partial,
    split,
    pick,
    lane_mask,
    well_mask,
    obs_all,
    sums,
    in_sem,
    halo_send,
    halo_recv,
    q_send,
    q_recv,
    obs_send,
    obs_recv,
    sum_send,
    sum_recv,
    data_send,
    data_recv,
):
    tile = lax.axis_index("tile")
    member = lax.axis_index("member")
    rows, layers, columns = sat.shape
    last = rows - 1
    wells_dev = obs_ref.shape[1]
    conns = cell_ref.shape[1]
    has_lo = tile > 0
    has_hi = tile < tiles - 1

    barrier = pltpu.get_barrier_semaphore()
    for d in range(1, tiles):
        pl.semaphore_signal(
            barrier, inc=1, device_id={"tile": lax.rem(tile + d, tiles)}, device_id_type=MESH
        )
    for d in range(1, members):
        pl.semaphore_signal(
            barrier, inc=1, device_id={"member": lax.rem(member + d, members)}, device_id_type=MESH
        )

    loads = [
        pltpu.make_async_copy(src, dst, in_sem.at[n])
        for n, (src, dst) in enumerate(
            (
                (sat_hbm.at[0, 0], sat.at[0]),
                (mob_hbm.at[0, 0], mob.at[0]),
                (sat_hbm.at[0, last], sat.at[last]),
                (mob_hbm.at[0, last], mob.at[last]),
                (sat_hbm.at[0, 1:last], sat.at[1:last]),
                (mob_hbm.at[0, 1:last], mob.at[1:last]),
                (qx_hbm.at[0], qx),
                (qz_hbm.at[0], qz),
                (qy_hbm.at[0], qy),
                (pore_hbm.at[0], pore),
                (obs_hbm, obs_ref),
                (cell_hbm, cell_ref),
                (well_hbm, well_ref),
                (factor_hbm, factor_ref),
            )
        )
    ]
    for load in loads:
        load.start()

    pl.semaphore_wait(barrier, tiles + members - 2)

    def exchange(src, dst_at, peers, axis, me, send_sem, recv_sem):
        copies = []
        for d in range(1, peers):
            copies.append(
                pltpu.make_async_remote_copy(
                    src_ref=src,
                    dst_ref=dst_at,
                    send_sem=send_sem.at[d - 1],
                    recv_sem=recv_sem.at[d - 1],
                    device_id={axis: lax.rem(me + d, peers)},
                    device_id_type=MESH,
                )
            )
            copies[-1].start()
        return copies

    q_copy = pltpu.make_async_remote_copy(
        src_ref=qx_hbm.at[0, 0],
        dst_ref=q_above,
        send_sem=q_send,
        recv_sem=q_recv,
        device_id={"tile": jnp.maximum(tile - 1, 0)},
        device_id_type=MESH,
    )

    def halo_copies(k):
        down = pltpu.make_async_remote_copy(
            src_ref=flow.at[k, 0],
            dst_ref=halo_hi.at[k],
            send_sem=halo_send.at[k, 0],
            recv_sem=halo_recv.at[k, 0],
            device_id={"tile": jnp.maximum(tile - 1, 0)},
            device_id_type=MESH,
        )
        up = pltpu.make_async_remote_copy(
            src_ref=flow.at[k, last],
            dst_ref=halo_lo.at[k],
            send_sem=halo_send.at[k, 1],
            recv_sem=halo_recv.at[k, 1],
            device_id={"tile": jnp.minimum(tile + 1, tiles - 1)},
            device_id_type=MESH,
        )
        return down, up

    halos = [halo_copies(k) for k in range(SUBSTEPS)]

    def send_halo(k):
        down, up = halos[k]

        @pl.when(has_lo)
        def _():
            down.start()

        @pl.when(has_hi)
        def _():
            up.start()

    def set_flow(k, i, value):
        flow[k, i] = value

    def set_split(i, value):
        high = value.astype(jnp.bfloat16)
        place = {0: 0, last: 1}[i] if isinstance(i, int) else i + 1
        at = pl.ds(pl.multiple_of(place * layers, layers), layers)
        split[at, 0:columns] = high
        split[at, columns : 2 * columns] = (value - high.astype(jnp.float32)).astype(jnp.bfloat16)

    for load in loads[0:4]:
        load.wait()
    set_flow(0, 0, frac(sat[0], mob[0]))
    set_flow(0, last, frac(sat[last], mob[last]))
    send_halo(0)

    @pl.when(has_lo)
    def _():
        q_copy.start()

    loads[10].wait()
    obs_all[tile] = jnp.ones((SUBLANES, LANES), jnp.float32)
    obs_all[tile, 0:SUBSTEPS, 0:wells_dev] = obs_ref[...]
    obs_copies = exchange(obs_all.at[tile], obs_all.at[tile], tiles, "tile", tile, obs_send, obs_recv)

    def first_flow(i, carry):
        set_flow(0, i, frac(sat[i], mob[i]))
        return carry

    for load in loads[4:6]:
        load.wait()
    lax.fori_loop(1, last, first_flow, 0)
    for load in loads[6:10]:
        load.wait()

    col_ids = lax.broadcasted_iota(jnp.int32, (layers, columns), 1)
    lay_ids = lax.broadcasted_iota(jnp.int32, (layers, columns), 0)

    def spread(k, i):
        here = flow[k, i]
        qz_i = jnp.where(lay_ids > 0, qz[i], 0.0)
        qy_i = jnp.where(col_ids > 0, qy[i], 0.0)
        face_z = face(qz_i, pltpu.roll(here, 1, 0), here)
        face_y = face(qy_i, pltpu.roll(here, 1, 1), here)
        return (pltpu.roll(face_z, layers - 1, 0) - face_z) + (
            pltpu.roll(face_y, columns - 1, 1) - face_y
        )

    def store(k, i, after):
        if k + 1 < SUBSTEPS:
            sat[i] = after
        else:
            new_ref[0, i] = after
        value = frac(after, mob[i])
        set_flow(k + 1, i, value)
        return value

    def set_masks():
        for load in loads[11:]:
            load.wait()
        lane_ids = lax.broadcasted_iota(jnp.int32, (conns, LANES), 1)
        cell_col = columns_of(cell_ref[...])
        row_col = lax.shift_right_logical(cell_col, columns.bit_length() - 1)
        spot = jnp.where(row_col < layers, row_col, row_col + layers)
        spot = jnp.where(row_col < last * layers, spot, row_col - (last - 1) * layers)
        for b in range(rows * layers // LANES):
            pick[:, b * LANES : (b + 1) * LANES] = jnp.where(
                spot == lane_ids + b * LANES, 1.0, 0.0
            ).astype(jnp.bfloat16)
        lane_mask[...] = jnp.where(
            cell_col - row_col * columns == lane_ids, columns_of(factor_ref[...]), 0.0
        )
        well_mask[...] = jnp.where(columns_of(well_ref[...]) == lane_ids, 1.0, 0.0)

    step_rates = []
    edge = 2 * layers

    def gather(start, stop):
        found = jnp.dot(
            pick[:, start:stop], split[start:stop, :], preferred_element_type=jnp.float32
        )
        return found[:, 0:columns] + found[:, columns : 2 * columns]

    def add_rates(found):
        rate = jnp.sum(found * lane_mask[...], axis=1, keepdims=True) * well_mask[...]
        step_rates.append(jnp.sum(rate, axis=0, keepdims=True))

    for k in range(SUBSTEPS):
        if k > 0:
            add_rates(gather(0, rows * layers))

        def inner(i, face_lo, k=k):
            face_hi = face(qx[i + 1], flow[k, i], flow[k, i + 1])
            after = sat[i] - pore[i] * ((face_hi - face_lo) + spread(k, i))
            set_split(i, store(k, i, after))
            return face_hi

        face_one = face(qx[1], flow[k, 0], flow[k, 1])
        face_last = lax.fori_loop(1, last, inner, face_one)
        partial[0] = sat[0] - pore[0] * (face_one + spread(k, 0))
        partial[1] = sat[last] - pore[last] * (spread(k, last) - face_last)
        if k == 0:
            set_masks()
        if k + 1 == SUBSTEPS:
            found_inner = gather(edge, rows * layers)

        down, up = halos[k]

        @pl.when(has_lo)
        def _():
            up.wait_recv()

        @pl.when(has_hi)
        def _():
            down.wait_recv()

        if k == 0:

            @pl.when(has_hi)
            def _():
                q_copy.wait_recv()

            @pl.when(jnp.logical_not(has_hi))
            def _():
                q_above[...] = jnp.zeros_like(q_above)

        below = jnp.where(has_lo, halo_lo[k], 0.0)
        above = jnp.where(has_hi, halo_hi[k], 0.0)
        qx_first = jnp.where(has_lo, qx[0], 0.0)
        value_first = store(k, 0, partial[0] + pore[0] * face(qx_first, below, flow[k, 0]))
        value_last = store(k, last, partial[1] - pore[last] * face(q_above[...], flow[k, last], above))
        if k + 1 < SUBSTEPS:
            send_halo(k + 1)
        set_split(0, value_first)
        set_split(last, value_last)
    add_rates(found_inner + gather(0, edge))
    step_rates.append(jnp.zeros((SUBLANES - SUBSTEPS, LANES), jnp.float32))
    sums[tile] = jnp.concatenate(step_rates, axis=0)
    sum_copies = exchange(sums.at[tile], sums.at[tile], tiles, "tile", tile, sum_send, sum_recv)
    for copy in obs_copies:
        copy.wait_recv()
    lane_row = lax.broadcasted_iota(jnp.int32, (SUBLANES, LANES), 1)
    obs_whole = obs_all[0]
    for t in range(1, tiles):
        moved = pltpu.roll(obs_all[t], t * wells_dev, 1)
        obs_whole = jnp.where(lane_row >= t * wells_dev, moved, obs_whole)
    for copy in sum_copies:
        copy.wait_recv()
    whole = sums[0]
    for t in range(1, tiles):
        whole = whole + sums[t]
    data[member] = whole / obs_whole
    data_copies = exchange(
        data.at[member], data.at[member], members, "member", member, data_send, data_recv
    )
    whole_ref[...] = whole
    for copy in data_copies:
        copy.wait_recv()

    for down, up in halos:

        @pl.when(has_lo)
        def _():
            down.wait_send()

        @pl.when(has_hi)
        def _():
            up.wait_send()

    @pl.when(has_lo)
    def _():
        q_copy.wait_send()

    for copy in obs_copies + sum_copies + data_copies:
        copy.wait_send()


def finish(new_ref, whole_ref, data, new_hbm, rates_hbm, gram_hbm, rates, gram, out_sem):
    tile = lax.axis_index("tile")
    member = lax.axis_index("member")
    members = data.shape[0]
    wells_dev = rates.shape[2]
    new_out = pltpu.make_async_copy(new_ref, new_hbm, out_sem.at[0])
    new_out.start()
    mine = pltpu.roll(whole_ref[...], lax.rem(LANES - tile * wells_dev, LANES), 1)
    for k in range(SUBSTEPS):
        rates[k] = mine[k : k + 1, 0:wells_dev]
    rates_out = pltpu.make_async_copy(rates, rates_hbm, out_sem.at[1])
    rates_out.start()
    mean = data[0]
    for m in range(1, members):
        mean = mean + data[m]
    mean = mean * (1.0 / members)
    own = data[member] - mean
    terms = jnp.concatenate(
        [jnp.sum(own * (data[m] - mean), axis=0, keepdims=True) for m in range(members)], axis=0
    )
    terms = jnp.sum(terms, axis=1, keepdims=True)
    square = (members, LANES)
    diagonal = lax.broadcasted_iota(jnp.int32, square, 0) == lax.broadcasted_iota(
        jnp.int32, square, 1
    )
    line = jnp.sum(jnp.where(diagonal, terms, 0.0), axis=0, keepdims=True)
    gram[...] = line[:, 0:members] / (members - 1.0)
    gram_out = pltpu.make_async_copy(gram, gram_hbm, out_sem.at[2])
    gram_out.start()
    new_out.wait()
    rates_out.wait()
    gram_out.wait()


def body(tiles, members, sat, mob, pore, qx, qy, qz, cell, well, factor, obs):
    block = sat.shape[1:]
    rows, layers, columns = block
    conns = cell.shape[0]
    wells_dev = obs.shape[0]
    f32 = jnp.float32
    dma = pltpu.SemaphoreType.DMA
    hbm_spec = pl.BlockSpec(memory_space=pltpu.HBM)
    vmem_spec = pl.BlockSpec(memory_space=pltpu.VMEM)
    new, whole, data = pl.pallas_call(
        functools.partial(kernel, tiles, members),
        out_shape=(
            pltpu.VMEM(sat.shape, f32),
            pltpu.VMEM((SUBLANES, LANES), f32),
            pltpu.VMEM((members, SUBLANES, LANES), f32),
        ),
        in_specs=[hbm_spec] * 10,
        out_specs=(vmem_spec,) * 3,
        scratch_shapes=[pltpu.VMEM(block, f32)] * 6
        + [
            pltpu.VMEM((1, conns), jnp.int32),
            pltpu.VMEM((1, conns), jnp.int32),
            pltpu.VMEM((1, conns), f32),
            pltpu.VMEM((SUBSTEPS, wells_dev), f32),
            pltpu.VMEM((SUBSTEPS + 1,) + block, f32),
            pltpu.VMEM((SUBSTEPS, layers, columns), f32),
            pltpu.VMEM((SUBSTEPS, layers, columns), f32),
            pltpu.VMEM((layers, columns), f32),
            pltpu.VMEM((2, layers, columns), f32),
            pltpu.VMEM((rows * layers, 2 * columns), jnp.bfloat16),
            pltpu.VMEM((conns, rows * layers), jnp.bfloat16),
            pltpu.VMEM((conns, LANES), f32),
            pltpu.VMEM((conns, LANES), f32),
            pltpu.VMEM((tiles, SUBLANES, LANES), f32),
            pltpu.VMEM((tiles, SUBLANES, LANES), f32),
            dma((14,)),
            dma((SUBSTEPS, 2)),
            dma((SUBSTEPS, 2)),
            dma(()),
            dma(()),
            dma((tiles - 1,)),
            dma((tiles - 1,)),
            dma((tiles - 1,)),
            dma((tiles - 1,)),
            dma((members - 1,)),
            dma((members - 1,)),
        ],
        compiler_params=pltpu.CompilerParams(
            collective_id=0, has_side_effects=True, vmem_limit_bytes=RUN_VMEM
        ),
        cost_estimate=pl.CostEstimate(
            flops=100 * SUBSTEPS * rows * layers * columns,
            bytes_accessed=28 * rows * layers * columns,
            transcendentals=0,
        ),
        name="transport",
    )(sat, mob, pore, qx, qy, qz, cell.reshape(1, -1), well.reshape(1, -1), factor.reshape(1, -1), obs.T)
    new, rates, gram = pl.pallas_call(
        finish,
        out_shape=(
            jax.ShapeDtypeStruct(sat.shape, f32),
            jax.ShapeDtypeStruct((SUBSTEPS, 1, wells_dev), f32),
            jax.ShapeDtypeStruct((1, members), f32),
        ),
        in_specs=[vmem_spec] * 3,
        out_specs=(hbm_spec,) * 3,
        scratch_shapes=[
            pltpu.VMEM((SUBSTEPS, 1, wells_dev), f32),
            pltpu.VMEM((1, members), f32),
            dma((3,)),
        ],
        compiler_params=pltpu.CompilerParams(vmem_limit_bytes=OUT_VMEM),
        name="finish",
    )(new, whole, data)
    return new, jnp.transpose(rates, (1, 2, 0)), gram


def solution(mesh):
    field = P("member", "tile", None, None)
    in_specs = (field,) * 6 + (P("tile"), P("tile"), P("tile"), P("tile", None))
    out_specs = (field, P("member", "tile", None), P("member", None))
    run = functools.partial(body, mesh.shape["tile"], mesh.shape["member"])
    return jax.shard_map(run, mesh=mesh, in_specs=in_specs, out_specs=out_specs, check_vma=False)
```

```python
import functools

import jax
import jax.numpy as jnp
from jax import lax
from jax.experimental import pallas as pl
from jax.experimental.pallas import tpu as pltpu
from jax.sharding import PartitionSpec as P

SUBSTEPS = 3
LANES = 128
SUBLANES = 8
MESH = pl.DeviceIdType.MESH
RUN_VMEM = 60 * 1024 * 1024
OUT_VMEM = 4 * 1024 * 1024


def frac(sat, mob):
    wet = sat * sat
    rest = 1.0 - sat
    whole = wet + mob * (rest * rest)
    inverse = pl.reciprocal(whole, approx=True)
    return wet * (inverse * (2.0 - whole * inverse))


def face(flux, below, here):
    return jnp.maximum(flux, 0.0) * below + jnp.minimum(flux, 0.0) * here


def columns_of(row):
    return jnp.transpose(jnp.broadcast_to(row, (LANES, row.shape[1])))


def kernel(
    tiles,
    members,
    sat_hbm,
    mob_hbm,
    pore_hbm,
    qx_hbm,
    qy_hbm,
    qz_hbm,
    cell_hbm,
    well_hbm,
    factor_hbm,
    obs_hbm,
    new_ref,
    parts,
    obs_all,
    sat,
    mob,
    pore,
    qx,
    qy,
    qz,
    cell_ref,
    well_ref,
    factor_ref,
    obs_ref,
    flow,
    halo_lo,
    halo_hi,
    q_above,
    partial,
    split,
    pick,
    lane_mask,
    well_mask,
    obs_line,
    in_sem,
    halo_send,
    halo_recv,
    q_send,
    q_recv,
    obs_send,
    obs_recv,
    part_send,
    part_recv,
):
    tile = lax.axis_index("tile")
    member = lax.axis_index("member")
    rows, layers, columns = sat.shape
    last = rows - 1
    wells_dev = obs_ref.shape[1]
    wells = wells_dev * tiles
    conns = cell_ref.shape[1]
    has_lo = tile > 0
    has_hi = tile < tiles - 1

    barrier = pltpu.get_barrier_semaphore()

    def peer(dm, dt):
        to_member = member + dm
        to_tile = tile + dt
        return {
            "member": jnp.where(to_member >= members, to_member - members, to_member),
            "tile": jnp.where(to_tile >= tiles, to_tile - tiles, to_tile),
        }

    def for_peers(act):
        for dt in range(1, tiles):
            act(0, dt)

        def far(dm, carry):
            for dt in range(tiles):
                act(dm, dt)
            return carry

        lax.fori_loop(1, members, far, 0)

    def greet(dm, dt):
        pl.semaphore_signal(barrier, inc=1, device_id=peer(dm, dt), device_id_type=MESH)

    for_peers(greet)

    loads = [
        pltpu.make_async_copy(src, dst, in_sem.at[n])
        for n, (src, dst) in enumerate(
            (
                (sat_hbm.at[0, 0], sat.at[0]),
                (mob_hbm.at[0, 0], mob.at[0]),
                (sat_hbm.at[0, last], sat.at[last]),
                (mob_hbm.at[0, last], mob.at[last]),
                (sat_hbm.at[0, 1:last], sat.at[1:last]),
                (mob_hbm.at[0, 1:last], mob.at[1:last]),
                (qx_hbm.at[0], qx),
                (qz_hbm.at[0], qz),
                (qy_hbm.at[0], qy),
                (pore_hbm.at[0], pore),
                (obs_hbm, obs_ref),
                (cell_hbm, cell_ref),
                (well_hbm, well_ref),
                (factor_hbm, factor_ref),
            )
        )
    ]
    for load in loads:
        load.start()

    pl.semaphore_wait(barrier, tiles * members - 1)

    def exchange(src, dst_at, peers, axis, me, send_sem, recv_sem):
        copies = []
        for d in range(1, peers):
            copies.append(
                pltpu.make_async_remote_copy(
                    src_ref=src,
                    dst_ref=dst_at,
                    send_sem=send_sem.at[d - 1],
                    recv_sem=recv_sem.at[d - 1],
                    device_id={axis: lax.rem(me + d, peers)},
                    device_id_type=MESH,
                )
            )
            copies[-1].start()
        return copies

    q_copy = pltpu.make_async_remote_copy(
        src_ref=qx_hbm.at[0, 0],
        dst_ref=q_above,
        send_sem=q_send,
        recv_sem=q_recv,
        device_id={"tile": jnp.maximum(tile - 1, 0)},
        device_id_type=MESH,
    )

    def halo_copies(k):
        down = pltpu.make_async_remote_copy(
            src_ref=flow.at[k, 0],
            dst_ref=halo_hi.at[k],
            send_sem=halo_send.at[k, 0],
            recv_sem=halo_recv.at[k, 0],
            device_id={"tile": jnp.maximum(tile - 1, 0)},
            device_id_type=MESH,
        )
        up = pltpu.make_async_remote_copy(
            src_ref=flow.at[k, last],
            dst_ref=halo_lo.at[k],
            send_sem=halo_send.at[k, 1],
            recv_sem=halo_recv.at[k, 1],
            device_id={"tile": jnp.minimum(tile + 1, tiles - 1)},
            device_id_type=MESH,
        )
        return down, up

    halos = [halo_copies(k) for k in range(SUBSTEPS)]

    def send_halo(k):
        down, up = halos[k]

        @pl.when(has_lo)
        def _():
            down.start()

        @pl.when(has_hi)
        def _():
            up.start()

    def set_flow(k, i, value):
        flow[k, i] = value

    def set_split(i, value):
        high = value.astype(jnp.bfloat16)
        place = {0: 0, last: 1}[i] if isinstance(i, int) else i + 1
        at = pl.ds(pl.multiple_of(place * layers, layers), layers)
        split[at, 0:columns] = high
        split[at, columns : 2 * columns] = (value - high.astype(jnp.float32)).astype(jnp.bfloat16)

    for load in loads[0:4]:
        load.wait()
    set_flow(0, 0, frac(sat[0], mob[0]))
    set_flow(0, last, frac(sat[last], mob[last]))
    send_halo(0)

    @pl.when(has_lo)
    def _():
        q_copy.start()

    loads[10].wait()
    obs_line[...] = jnp.zeros_like(obs_line)
    obs_line[0:SUBSTEPS, 0:wells_dev] = obs_ref[...]
    lines = [jnp.zeros((1, LANES), jnp.float32)] * parts.shape[2]
    for k in range(SUBSTEPS):
        row, lane = divmod(k * wells, LANES)
        lines[row] = lines[row] + pltpu.roll(
            obs_line[k : k + 1, :], lane + tile * wells_dev, 1
        )
    packed = jnp.concatenate(lines, axis=0)
    obs_all[tile] = jnp.where(packed == 0.0, 1.0, packed)
    obs_copies = exchange(obs_all.at[tile], obs_all.at[tile], tiles, "tile", tile, obs_send, obs_recv)

    def first_flow(i, carry):
        set_flow(0, i, frac(sat[i], mob[i]))
        return carry

    for load in loads[4:6]:
        load.wait()
    lax.fori_loop(1, last, first_flow, 0)
    for load in loads[6:10]:
        load.wait()

    col_ids = lax.broadcasted_iota(jnp.int32, (layers, columns), 1)
    lay_ids = lax.broadcasted_iota(jnp.int32, (layers, columns), 0)

    def spread(k, i):
        here = flow[k, i]
        qz_i = jnp.where(lay_ids > 0, qz[i], 0.0)
        qy_i = jnp.where(col_ids > 0, qy[i], 0.0)
        face_z = face(qz_i, pltpu.roll(here, 1, 0), here)
        face_y = face(qy_i, pltpu.roll(here, 1, 1), here)
        return (pltpu.roll(face_z, layers - 1, 0) - face_z) + (
            pltpu.roll(face_y, columns - 1, 1) - face_y
        )

    def store(k, i, after):
        if k + 1 < SUBSTEPS:
            sat[i] = after
        else:
            new_ref[0, i] = after
        value = frac(after, mob[i])
        set_flow(k + 1, i, value)
        return value

    def set_masks():
        for load in loads[11:]:
            load.wait()
        lane_ids = lax.broadcasted_iota(jnp.int32, (conns, LANES), 1)
        cell_col = columns_of(cell_ref[...])
        row_col = lax.shift_right_logical(cell_col, columns.bit_length() - 1)
        spot = jnp.where(row_col < layers, row_col, row_col + layers)
        spot = jnp.where(row_col < last * layers, spot, row_col - (last - 1) * layers)
        for b in range(rows * layers // LANES):
            pick[:, b * LANES : (b + 1) * LANES] = jnp.where(
                spot == lane_ids + b * LANES, 1.0, 0.0
            ).astype(jnp.bfloat16)
        lane_mask[...] = jnp.where(
            cell_col - row_col * columns == lane_ids, columns_of(factor_ref[...]), 0.0
        )
        well_mask[...] = jnp.where(columns_of(well_ref[...]) == lane_ids, 1.0, 0.0)

    step_rates = []
    edge = 2 * layers

    def gather(start, stop):
        found = jnp.dot(
            pick[:, start:stop], split[start:stop, :], preferred_element_type=jnp.float32
        )
        return found[:, 0:columns] + found[:, columns : 2 * columns]

    def add_rates(found):
        rate = jnp.sum(found * lane_mask[...], axis=1, keepdims=True) * well_mask[...]
        step_rates.append(jnp.sum(rate, axis=0, keepdims=True))

    for k in range(SUBSTEPS):
        if k > 0:
            add_rates(gather(0, rows * layers))

        def inner(i, face_lo, k=k):
            face_hi = face(qx[i + 1], flow[k, i], flow[k, i + 1])
            after = sat[i] - pore[i] * ((face_hi - face_lo) + spread(k, i))
            set_split(i, store(k, i, after))
            return face_hi

        face_one = face(qx[1], flow[k, 0], flow[k, 1])
        face_last = lax.fori_loop(1, last, inner, face_one)
        partial[0] = sat[0] - pore[0] * (face_one + spread(k, 0))
        partial[1] = sat[last] - pore[last] * (spread(k, last) - face_last)
        if k == 0:
            set_masks()
        if k + 1 == SUBSTEPS:
            found_inner = gather(edge, rows * layers)

        down, up = halos[k]

        @pl.when(has_lo)
        def _():
            up.wait_recv()

        @pl.when(has_hi)
        def _():
            down.wait_recv()

        if k == 0:

            @pl.when(has_hi)
            def _():
                q_copy.wait_recv()

            @pl.when(jnp.logical_not(has_hi))
            def _():
                q_above[...] = jnp.zeros_like(q_above)

        below = jnp.where(has_lo, halo_lo[k], 0.0)
        above = jnp.where(has_hi, halo_hi[k], 0.0)
        qx_first = jnp.where(has_lo, qx[0], 0.0)
        value_first = store(k, 0, partial[0] + pore[0] * face(qx_first, below, flow[k, 0]))
        value_last = store(k, last, partial[1] - pore[last] * face(q_above[...], flow[k, last], above))
        if k + 1 < SUBSTEPS:
            send_halo(k + 1)
        set_split(0, value_first)
        set_split(last, value_last)
    add_rates(found_inner + gather(0, edge))
    lines = [jnp.zeros((1, LANES), jnp.float32)] * parts.shape[2]
    for k in range(SUBSTEPS):
        row, lane = divmod(k * wells, LANES)
        lines[row] = lines[row] + (pltpu.roll(step_rates[k], lane, 1) if lane else step_rates[k])
    parts[tile, member] = jnp.concatenate(lines, axis=0)

    def part_copy(dm, dt):
        n = dm * tiles + dt - 1
        return pltpu.make_async_remote_copy(
            src_ref=parts.at[tile, member],
            dst_ref=parts.at[tile, member],
            send_sem=part_send.at[n],
            recv_sem=part_recv.at[n],
            device_id=peer(dm, dt),
            device_id_type=MESH,
        )

    for_peers(lambda dm, dt: part_copy(dm, dt).start())
    for copy in obs_copies:
        copy.wait_recv()
    for_peers(lambda dm, dt: part_copy(dm, dt).wait_recv())

    for down, up in halos:

        @pl.when(has_lo)
        def _():
            down.wait_send()

        @pl.when(has_hi)
        def _():
            up.wait_send()

    @pl.when(has_lo)
    def _():
        q_copy.wait_send()

    for copy in obs_copies:
        copy.wait_send()
    for_peers(lambda dm, dt: part_copy(dm, dt).wait_send())


def finish(new_ref, parts, obs_all, new_hbm, rates_hbm, gram_hbm, rates, gram, out_sem):
    tile = lax.axis_index("tile")
    member = lax.axis_index("member")
    tiles, members = parts.shape[0:2]
    wells_dev = rates.shape[2]
    wells = wells_dev * tiles
    new_out = pltpu.make_async_copy(new_ref, new_hbm, out_sem.at[0])
    new_out.start()

    def tile_sum(m):
        whole = parts[0, m]
        for t in range(1, tiles):
            whole = whole + parts[t, m]
        return whole

    mine = tile_sum(member)
    for k in range(SUBSTEPS):
        row, lane = divmod(k * wells, LANES)
        moved = pltpu.roll(
            mine[row : row + 1], lax.rem(2 * LANES - lane - tile * wells_dev, LANES), 1
        )
        rates[k] = moved[:, 0:wells_dev]
    rates_out = pltpu.make_async_copy(rates, rates_hbm, out_sem.at[1])
    rates_out.start()
    obs = obs_all[0]
    for t in range(1, tiles):
        obs = obs * obs_all[t]
    data = [tile_sum(m) / obs for m in range(members)]
    mean = data[0]
    for m in range(1, members):
        mean = mean + data[m]
    mean = mean * (1.0 / members)
    own = mine / obs - mean
    terms = jnp.concatenate(
        [jnp.sum(own * (data[m] - mean), axis=0, keepdims=True) for m in range(members)], axis=0
    )
    terms = jnp.sum(terms, axis=1, keepdims=True)
    square = (members, LANES)
    diagonal = lax.broadcasted_iota(jnp.int32, square, 0) == lax.broadcasted_iota(
        jnp.int32, square, 1
    )
    line = jnp.sum(jnp.where(diagonal, terms, 0.0), axis=0, keepdims=True)
    gram[...] = line[:, 0:members] / (members - 1.0)
    gram_out = pltpu.make_async_copy(gram, gram_hbm, out_sem.at[2])
    gram_out.start()
    new_out.wait()
    rates_out.wait()
    gram_out.wait()


def body(tiles, members, sat, mob, pore, qx, qy, qz, cell, well, factor, obs):
    block = sat.shape[1:]
    rows, layers, columns = block
    conns = cell.shape[0]
    wells_dev = obs.shape[0]
    f32 = jnp.float32
    dma = pltpu.SemaphoreType.DMA
    hbm_spec = pl.BlockSpec(memory_space=pltpu.HBM)
    vmem_spec = pl.BlockSpec(memory_space=pltpu.VMEM)
    lines = -(-SUBSTEPS * wells_dev * tiles // LANES)
    new, parts, obs_all = pl.pallas_call(
        functools.partial(kernel, tiles, members),
        out_shape=(
            pltpu.VMEM(sat.shape, f32),
            pltpu.VMEM((tiles, members, lines, LANES), f32),
            pltpu.VMEM((tiles, lines, LANES), f32),
        ),
        in_specs=[hbm_spec] * 10,
        out_specs=(vmem_spec,) * 3,
        scratch_shapes=[pltpu.VMEM(block, f32)] * 6
        + [
            pltpu.VMEM((1, conns), jnp.int32),
            pltpu.VMEM((1, conns), jnp.int32),
            pltpu.VMEM((1, conns), f32),
            pltpu.VMEM((SUBSTEPS, wells_dev), f32),
            pltpu.VMEM((SUBSTEPS + 1,) + block, f32),
            pltpu.VMEM((SUBSTEPS, layers, columns), f32),
            pltpu.VMEM((SUBSTEPS, layers, columns), f32),
            pltpu.VMEM((layers, columns), f32),
            pltpu.VMEM((2, layers, columns), f32),
            pltpu.VMEM((rows * layers, 2 * columns), jnp.bfloat16),
            pltpu.VMEM((conns, rows * layers), jnp.bfloat16),
            pltpu.VMEM((conns, LANES), f32),
            pltpu.VMEM((conns, LANES), f32),
            pltpu.VMEM((SUBLANES, LANES), f32),
            dma((14,)),
            dma((SUBSTEPS, 2)),
            dma((SUBSTEPS, 2)),
            dma(()),
            dma(()),
            dma((tiles - 1,)),
            dma((tiles - 1,)),
            dma((tiles * members - 1,)),
            dma((tiles * members - 1,)),
        ],
        compiler_params=pltpu.CompilerParams(
            collective_id=0, has_side_effects=True, vmem_limit_bytes=RUN_VMEM
        ),
        cost_estimate=pl.CostEstimate(
            flops=100 * SUBSTEPS * rows * layers * columns,
            bytes_accessed=28 * rows * layers * columns,
            transcendentals=0,
        ),
        name="transport",
    )(sat, mob, pore, qx, qy, qz, cell.reshape(1, -1), well.reshape(1, -1), factor.reshape(1, -1), obs.T)
    new, rates, gram = pl.pallas_call(
        finish,
        out_shape=(
            jax.ShapeDtypeStruct(sat.shape, f32),
            jax.ShapeDtypeStruct((SUBSTEPS, 1, wells_dev), f32),
            jax.ShapeDtypeStruct((1, members), f32),
        ),
        in_specs=[vmem_spec] * 3,
        out_specs=(hbm_spec,) * 3,
        scratch_shapes=[
            pltpu.VMEM((SUBSTEPS, 1, wells_dev), f32),
            pltpu.VMEM((1, members), f32),
            dma((3,)),
        ],
        compiler_params=pltpu.CompilerParams(vmem_limit_bytes=OUT_VMEM),
        name="finish",
    )(new, parts, obs_all)
    return new, jnp.transpose(rates, (1, 2, 0)), gram


def solution(mesh):
    field = P("member", "tile", None, None)
    in_specs = (field,) * 6 + (P("tile"), P("tile"), P("tile"), P("tile", None))
    out_specs = (field, P("member", "tile", None), P("member", None))
    run = functools.partial(body, mesh.shape["tile"], mesh.shape["member"])
    return jax.shard_map(run, mesh=mesh, in_specs=in_specs, out_specs=out_specs, check_vma=False)
```

```python
import functools

import jax
import jax.numpy as jnp
from jax import lax
from jax.experimental import pallas as pl
from jax.experimental.pallas import tpu as pltpu
from jax.sharding import PartitionSpec as P

SUBSTEPS = 3
LANES = 128
SUBLANES = 8
MESH = pl.DeviceIdType.MESH
RUN_VMEM = 60 * 1024 * 1024
OUT_VMEM = 4 * 1024 * 1024


def frac(sat, mob):
    wet = sat * sat
    rest = 1.0 - sat
    whole = wet + mob * (rest * rest)
    inverse = pl.reciprocal(whole, approx=True)
    return wet * (inverse * (2.0 - whole * inverse))


def face(flux, below, here):
    return jnp.maximum(flux, 0.0) * below + jnp.minimum(flux, 0.0) * here


def columns_of(row):
    return jnp.transpose(jnp.broadcast_to(row, (LANES, row.shape[1])))


def kernel(
    tiles,
    members,
    sat_hbm,
    mob_hbm,
    pore_hbm,
    qx_hbm,
    qy_hbm,
    qz_hbm,
    cell_hbm,
    well_hbm,
    factor_hbm,
    obs_hbm,
    new_ref,
    parts,
    obs_all,
    sat,
    mob,
    pore,
    qx,
    qy,
    qz,
    cell_ref,
    well_ref,
    factor_ref,
    obs_ref,
    flow,
    beside,
    behind,
    sat_beside,
    sat_edge,
    fixed,
    q_below,
    q_above,
    partial,
    split,
    pick,
    lane_mask,
    well_mask,
    obs_line,
    in_sem,
    halo_send,
    halo_recv,
    obs_send,
    obs_recv,
    part_send,
    part_recv,
):
    tile = lax.axis_index("tile")
    member = lax.axis_index("member")
    rows, layers, columns = sat.shape
    last = rows - 1
    wells_dev = obs_ref.shape[1]
    wells = wells_dev * tiles
    conns = cell_ref.shape[1]
    has_lo = tile > 0
    has_hi = tile < tiles - 1

    barrier = pltpu.get_barrier_semaphore()

    def peer(dm, dt):
        to_member = member + dm
        to_tile = tile + dt
        return {
            "member": jnp.where(to_member >= members, to_member - members, to_member),
            "tile": jnp.where(to_tile >= tiles, to_tile - tiles, to_tile),
        }

    def for_peers(act):
        for dt in range(1, tiles):
            act(0, dt)

        def far(dm, carry):
            for dt in range(tiles):
                act(dm, dt)
            return carry

        lax.fori_loop(1, members, far, 0)

    def greet(dm, dt):
        pl.semaphore_signal(barrier, inc=1, device_id=peer(dm, dt), device_id_type=MESH)

    for_peers(greet)

    loads = [
        pltpu.make_async_copy(src, dst, in_sem.at[n])
        for n, (src, dst) in enumerate(
            (
                (sat_hbm.at[0, 0], sat.at[0]),
                (mob_hbm.at[0, 0], mob.at[0]),
                (sat_hbm.at[0, last], sat.at[last]),
                (mob_hbm.at[0, last], mob.at[last]),
                (sat_hbm.at[0, 1:last], sat.at[1:last]),
                (mob_hbm.at[0, 1:last], mob.at[1:last]),
                (qx_hbm.at[0], qx),
                (qz_hbm.at[0], qz),
                (qy_hbm.at[0], qy),
                (pore_hbm.at[0], pore),
                (obs_hbm, obs_ref),
                (cell_hbm, cell_ref),
                (well_hbm, well_ref),
                (factor_hbm, factor_ref),
            )
        )
    ]
    for load in loads:
        load.start()

    pl.semaphore_wait(barrier, tiles * members - 1)

    def exchange(src, dst_at, peers, axis, me, send_sem, recv_sem):
        copies = []
        for d in range(1, peers):
            copies.append(
                pltpu.make_async_remote_copy(
                    src_ref=src,
                    dst_ref=dst_at,
                    send_sem=send_sem.at[d - 1],
                    recv_sem=recv_sem.at[d - 1],
                    device_id={axis: lax.rem(me + d, peers)},
                    device_id_type=MESH,
                )
            )
            copies[-1].start()
        return copies

    def to_side(n, up, src, dst):
        side = 0 if up else 1
        beyond = jnp.minimum(tile + 1, tiles - 1) if up else jnp.maximum(tile - 1, 0)
        return pltpu.make_async_remote_copy(
            src_ref=src,
            dst_ref=dst,
            send_sem=halo_send.at[side, n],
            recv_sem=halo_recv.at[side, n],
            device_id={"tile": beyond},
            device_id_type=MESH,
        )

    ups = [
        to_side(0, True, flow.at[0, last], beside.at[0]),
        to_side(1, True, qx_hbm.at[0, last], q_below),
    ]
    downs = [
        to_side(0, False, flow.at[0, 0], beside.at[1]),
        to_side(1, False, qx_hbm.at[0, 0:2], q_above),
    ]
    for n, field in enumerate((mob_hbm, pore_hbm, qz_hbm, qy_hbm)):
        ups.append(to_side(n + 2, True, field.at[0, last], fixed.at[0, n]))
        downs.append(to_side(n + 2, False, field.at[0, 0], fixed.at[1, n]))
    ups.append(to_side(6, True, flow.at[1, last - 1], behind.at[0]))
    downs.append(to_side(6, False, flow.at[1, 1], behind.at[1]))
    ups.append(to_side(7, True, sat_edge.at[1], sat_beside.at[0]))
    downs.append(to_side(7, False, sat_edge.at[0], sat_beside.at[1]))

    def send(start, stop):
        @pl.when(has_lo)
        def _():
            for copy in downs[start:stop]:
                copy.start()

        @pl.when(has_hi)
        def _():
            for copy in ups[start:stop]:
                copy.start()

    def receive(start, stop):
        @pl.when(has_lo)
        def _():
            for copy in ups[start:stop]:
                copy.wait_recv()

        @pl.when(has_hi)
        def _():
            for copy in downs[start:stop]:
                copy.wait_recv()

    def set_flow(k, i, value):
        flow[k, i] = value

    def set_split(k, i, value):
        high = value.astype(jnp.bfloat16)
        if isinstance(i, int):
            place = {0: 0, last: 1, 1: 2, last - 1: 3}[i]
        else:
            place = jnp.where(i == 1, 2, jnp.where(i == last - 1, 3, i + 2))
        at = pl.ds(pl.multiple_of(place * layers, layers), layers)
        split[k % 2, at, 0:columns] = high
        split[k % 2, at, columns : 2 * columns] = (value - high.astype(jnp.float32)).astype(jnp.bfloat16)

    for load in loads[0:4]:
        load.wait()
    set_flow(0, 0, frac(sat[0], mob[0]))
    set_flow(0, last, frac(sat[last], mob[last]))
    send(0, 6)

    loads[10].wait()
    obs_line[...] = jnp.zeros_like(obs_line)
    obs_line[0:SUBSTEPS, 0:wells_dev] = obs_ref[...]
    lines = [jnp.zeros((1, LANES), jnp.float32)] * parts.shape[2]
    for k in range(SUBSTEPS):
        row, lane = divmod(k * wells, LANES)
        lines[row] = lines[row] + pltpu.roll(
            obs_line[k : k + 1, :], lane + tile * wells_dev, 1
        )
    packed = jnp.concatenate(lines, axis=0)
    obs_all[tile] = jnp.where(packed == 0.0, 1.0, packed)
    obs_copies = exchange(obs_all.at[tile], obs_all.at[tile], tiles, "tile", tile, obs_send, obs_recv)

    def first_flow(i, carry):
        set_flow(0, i, frac(sat[i], mob[i]))
        return carry

    for load in loads[4:6]:
        load.wait()
    lax.fori_loop(1, last, first_flow, 0)
    for load in loads[6:10]:
        load.wait()

    col_ids = lax.broadcasted_iota(jnp.int32, (layers, columns), 1)
    lay_ids = lax.broadcasted_iota(jnp.int32, (layers, columns), 0)

    def spread_of(here, qz_i, qy_i):
        qz_i = jnp.where(lay_ids > 0, qz_i, 0.0)
        qy_i = jnp.where(col_ids > 0, qy_i, 0.0)
        face_z = face(qz_i, pltpu.roll(here, 1, 0), here)
        face_y = face(qy_i, pltpu.roll(here, 1, 1), here)
        return (pltpu.roll(face_z, layers - 1, 0) - face_z) + (
            pltpu.roll(face_y, columns - 1, 1) - face_y
        )

    def spread(k, i):
        return spread_of(flow[k, i], qz[i], qy[i])

    def face_at(k, i):
        return face(qx[i], flow[k, i - 1], flow[k, i])

    def store(k, i, after):
        if k + 1 < SUBSTEPS:
            sat[i] = after
        else:
            new_ref[0, i] = after
        value = frac(after, mob[i])
        set_flow(k + 1, i, value)
        return value

    def set_masks():
        for load in loads[11:]:
            load.wait()
        lane_ids = lax.broadcasted_iota(jnp.int32, (conns, LANES), 1)
        cell_col = columns_of(cell_ref[...])
        row_col = lax.shift_right_logical(cell_col, columns.bit_length() - 1)
        spot = jnp.where(row_col < layers, row_col, row_col + layers)
        spot = jnp.where(row_col < 2 * layers, spot, row_col + 2 * layers)
        spot = jnp.where(row_col < (last - 1) * layers, spot, row_col - (last - 4) * layers)
        spot = jnp.where(row_col < last * layers, spot, row_col - (last - 1) * layers)
        for b in range(rows * layers // LANES):
            pick[:, b * LANES : (b + 1) * LANES] = jnp.where(
                spot == lane_ids + b * LANES, 1.0, 0.0
            ).astype(jnp.bfloat16)
        lane_mask[...] = jnp.where(
            cell_col - row_col * columns == lane_ids, columns_of(factor_ref[...]), 0.0
        )
        well_mask[...] = jnp.where(columns_of(well_ref[...]) == lane_ids, 1.0, 0.0)

    step_rates = []
    two = 2 * layers
    four = 4 * layers
    cells = rows * layers

    def gather(k, start, stop):
        found = jnp.dot(
            pick[:, start:stop], split[k % 2, start:stop, :], preferred_element_type=jnp.float32
        )
        return found[:, 0:columns] + found[:, columns : 2 * columns]

    def add_rates(found):
        rate = jnp.sum(found * lane_mask[...], axis=1, keepdims=True) * well_mask[...]
        step_rates.append(jnp.sum(rate, axis=0, keepdims=True))

    def inner_rows(k, start, stop):
        def inner(i, face_lo):
            face_hi = face(qx[i + 1], flow[k, i], flow[k, i + 1])
            value = store(k, i, sat[i] - pore[i] * ((face_hi - face_lo) + spread(k, i)))
            set_split(k, i, value)
            return face_hi

        face_first = face_at(k, start)
        return face_first, lax.fori_loop(start, stop, inner, face_first)

    face_lo, face_hi = inner_rows(0, 1, last)
    send(6, 7)
    partial[0] = sat[0] - pore[0] * (face_lo + spread(0, 0))
    partial[1] = sat[last] - pore[last] * (spread(0, last) - face_hi)
    qx_first = jnp.where(has_lo, qx[0], 0.0)
    set_masks()
    receive(0, 2)

    @pl.when(jnp.logical_not(has_hi))
    def _():
        q_above[...] = jnp.zeros_like(q_above)

    below = jnp.where(has_lo, beside[0], 0.0)
    above = jnp.where(has_hi, beside[1], 0.0)
    first = partial[0] + pore[0] * face(qx_first, below, flow[0, 0])
    final = partial[1] - pore[last] * face(q_above[0], flow[0, last], above)
    sat_edge[0] = first
    sat_edge[1] = final
    send(7, 8)
    set_split(0, 0, store(0, 0, first))
    set_split(0, last, store(0, last, final))

    add_rates(gather(0, 0, cells))
    face_lo, face_hi = inner_rows(1, 1, last)
    partial[0] = sat[0] - pore[0] * (face_lo + spread(1, 0))
    partial[1] = sat[last] - pore[last] * (spread(1, last) - face_hi)
    found_second = gather(1, two, cells)
    face_lo, face_hi = inner_rows(2, 2, last - 1)
    partial[2] = sat[1] - pore[1] * (face_lo + spread(2, 1))
    partial[3] = sat[last - 1] - pore[last - 1] * (spread(2, last - 1) - face_hi)
    found_third = gather(2, four, cells)
    receive(2, 8)

    def advance_beside(side, here, lower, upper):
        mob_i, pore_i, qz_i, qy_i = (fixed[side, n] for n in range(4))
        total = (upper - lower) + spread_of(here, qz_i, qy_i)
        return frac(sat_beside[side] - pore_i * total, mob_i)

    flow_lo = frac(sat_beside[0], fixed[0, 0])
    flow_hi = frac(sat_beside[1], fixed[1, 0])
    face_lo = face(qx_first, jnp.where(has_lo, flow_lo, 0.0), flow[1, 0])
    face_hi = face(q_above[0], flow[1, last], jnp.where(has_hi, flow_hi, 0.0))
    set_split(1, 0, store(1, 0, partial[0] + pore[0] * face_lo))
    set_split(1, last, store(1, last, partial[1] - pore[last] * face_hi))
    below = advance_beside(0, flow_lo, face(q_below[...], behind[0], flow_lo), face_lo)
    above = advance_beside(1, flow_hi, face_hi, face(q_above[1], flow_hi, behind[1]))

    face_lo = face(qx_first, jnp.where(has_lo, below, 0.0), flow[2, 0])
    face_hi = face(q_above[0], flow[2, last], jnp.where(has_hi, above, 0.0))
    face_one = face_at(2, 1)
    face_last = face_at(2, last)
    for i, after in (
        (0, sat[0] - pore[0] * ((face_one - face_lo) + spread(2, 0))),
        (1, partial[2] + pore[1] * face_one),
        (last - 1, partial[3] - pore[last - 1] * face_last),
        (last, sat[last] - pore[last] * ((face_hi - face_last) + spread(2, last))),
    ):
        set_split(2, i, store(2, i, after))
    add_rates(found_second + gather(1, 0, two))
    add_rates(found_third + gather(2, 0, four))

    lines = [jnp.zeros((1, LANES), jnp.float32)] * parts.shape[2]
    for k in range(SUBSTEPS):
        row, lane = divmod(k * wells, LANES)
        lines[row] = lines[row] + (pltpu.roll(step_rates[k], lane, 1) if lane else step_rates[k])
    parts[tile, member] = jnp.concatenate(lines, axis=0)

    def part_copy(dm, dt):
        n = dm * tiles + dt - 1
        return pltpu.make_async_remote_copy(
            src_ref=parts.at[tile, member],
            dst_ref=parts.at[tile, member],
            send_sem=part_send.at[n],
            recv_sem=part_recv.at[n],
            device_id=peer(dm, dt),
            device_id_type=MESH,
        )

    for_peers(lambda dm, dt: part_copy(dm, dt).start())
    for copy in obs_copies:
        copy.wait_recv()
    for_peers(lambda dm, dt: part_copy(dm, dt).wait_recv())

    @pl.when(has_lo)
    def _():
        for copy in downs:
            copy.wait_send()

    @pl.when(has_hi)
    def _():
        for copy in ups:
            copy.wait_send()

    for copy in obs_copies:
        copy.wait_send()
    for_peers(lambda dm, dt: part_copy(dm, dt).wait_send())


def finish(new_ref, parts, obs_all, new_hbm, rates_hbm, gram_hbm, rates, gram, out_sem):
    tile = lax.axis_index("tile")
    member = lax.axis_index("member")
    tiles, members = parts.shape[0:2]
    wells_dev = rates.shape[2]
    wells = wells_dev * tiles
    new_out = pltpu.make_async_copy(new_ref, new_hbm, out_sem.at[0])
    new_out.start()

    def tile_sum(m):
        whole = parts[0, m]
        for t in range(1, tiles):
            whole = whole + parts[t, m]
        return whole

    mine = tile_sum(member)
    for k in range(SUBSTEPS):
        row, lane = divmod(k * wells, LANES)
        moved = pltpu.roll(
            mine[row : row + 1], lax.rem(2 * LANES - lane - tile * wells_dev, LANES), 1
        )
        rates[k] = moved[:, 0:wells_dev]
    rates_out = pltpu.make_async_copy(rates, rates_hbm, out_sem.at[1])
    rates_out.start()
    obs = obs_all[0]
    for t in range(1, tiles):
        obs = obs * obs_all[t]
    data = [tile_sum(m) / obs for m in range(members)]
    mean = data[0]
    for m in range(1, members):
        mean = mean + data[m]
    mean = mean * (1.0 / members)
    own = mine / obs - mean
    terms = jnp.concatenate(
        [jnp.sum(own * (data[m] - mean), axis=0, keepdims=True) for m in range(members)], axis=0
    )
    terms = jnp.sum(terms, axis=1, keepdims=True)
    square = (members, LANES)
    diagonal = lax.broadcasted_iota(jnp.int32, square, 0) == lax.broadcasted_iota(
        jnp.int32, square, 1
    )
    line = jnp.sum(jnp.where(diagonal, terms, 0.0), axis=0, keepdims=True)
    gram[...] = line[:, 0:members] / (members - 1.0)
    gram_out = pltpu.make_async_copy(gram, gram_hbm, out_sem.at[2])
    gram_out.start()
    new_out.wait()
    rates_out.wait()
    gram_out.wait()


def body(tiles, members, sat, mob, pore, qx, qy, qz, cell, well, factor, obs):
    block = sat.shape[1:]
    rows, layers, columns = block
    conns = cell.shape[0]
    wells_dev = obs.shape[0]
    f32 = jnp.float32
    dma = pltpu.SemaphoreType.DMA
    hbm_spec = pl.BlockSpec(memory_space=pltpu.HBM)
    vmem_spec = pl.BlockSpec(memory_space=pltpu.VMEM)
    lines = -(-SUBSTEPS * wells_dev * tiles // LANES)
    new, parts, obs_all = pl.pallas_call(
        functools.partial(kernel, tiles, members),
        out_shape=(
            pltpu.VMEM(sat.shape, f32),
            pltpu.VMEM((tiles, members, lines, LANES), f32),
            pltpu.VMEM((tiles, lines, LANES), f32),
        ),
        in_specs=[hbm_spec] * 10,
        out_specs=(vmem_spec,) * 3,
        scratch_shapes=[pltpu.VMEM(block, f32)] * 6
        + [
            pltpu.VMEM((1, conns), jnp.int32),
            pltpu.VMEM((1, conns), jnp.int32),
            pltpu.VMEM((1, conns), f32),
            pltpu.VMEM((SUBSTEPS, wells_dev), f32),
            pltpu.VMEM((SUBSTEPS + 1,) + block, f32),
            pltpu.VMEM((2, layers, columns), f32),
            pltpu.VMEM((2, layers, columns), f32),
            pltpu.VMEM((2, layers, columns), f32),
            pltpu.VMEM((2, layers, columns), f32),
            pltpu.VMEM((2, 4, layers, columns), f32),
            pltpu.VMEM((layers, columns), f32),
            pltpu.VMEM((2, layers, columns), f32),
            pltpu.VMEM((4, layers, columns), f32),
            pltpu.VMEM((2, rows * layers, 2 * columns), jnp.bfloat16),
            pltpu.VMEM((conns, rows * layers), jnp.bfloat16),
            pltpu.VMEM((conns, LANES), f32),
            pltpu.VMEM((conns, LANES), f32),
            pltpu.VMEM((SUBLANES, LANES), f32),
            dma((14,)),
            dma((2, 8)),
            dma((2, 8)),
            dma((tiles - 1,)),
            dma((tiles - 1,)),
            dma((tiles * members - 1,)),
            dma((tiles * members - 1,)),
        ],
        compiler_params=pltpu.CompilerParams(
            collective_id=0, has_side_effects=True, vmem_limit_bytes=RUN_VMEM
        ),
        cost_estimate=pl.CostEstimate(
            flops=100 * SUBSTEPS * rows * layers * columns,
            bytes_accessed=28 * rows * layers * columns,
            transcendentals=0,
        ),
        name="transport",
    )(sat, mob, pore, qx, qy, qz, cell.reshape(1, -1), well.reshape(1, -1), factor.reshape(1, -1), obs.T)
    new, rates, gram = pl.pallas_call(
        finish,
        out_shape=(
            jax.ShapeDtypeStruct(sat.shape, f32),
            jax.ShapeDtypeStruct((SUBSTEPS, 1, wells_dev), f32),
            jax.ShapeDtypeStruct((1, members), f32),
        ),
        in_specs=[vmem_spec] * 3,
        out_specs=(hbm_spec,) * 3,
        scratch_shapes=[
            pltpu.VMEM((SUBSTEPS, 1, wells_dev), f32),
            pltpu.VMEM((1, members), f32),
            dma((3,)),
        ],
        compiler_params=pltpu.CompilerParams(vmem_limit_bytes=OUT_VMEM),
        name="finish",
    )(new, parts, obs_all)
    return new, jnp.transpose(rates, (1, 2, 0)), gram


def solution(mesh):
    field = P("member", "tile", None, None)
    in_specs = (field,) * 6 + (P("tile"), P("tile"), P("tile"), P("tile", None))
    out_specs = (field, P("member", "tile", None), P("member", None))
    run = functools.partial(body, mesh.shape["tile"], mesh.shape["member"])
    return jax.shard_map(run, mesh=mesh, in_specs=in_specs, out_specs=out_specs, check_vma=False)
```

```python
import functools

import jax
import jax.numpy as jnp
from jax import lax
from jax.experimental import pallas as pl
from jax.experimental.pallas import tpu as pltpu
from jax.sharding import PartitionSpec as P

SUBSTEPS = 3
LANES = 128
SUBLANES = 8
MESH = pl.DeviceIdType.MESH
RUN_VMEM = 60 * 1024 * 1024
OUT_VMEM = 4 * 1024 * 1024


def frac(sat, mob):
    wet = sat * sat
    rest = 1.0 - sat
    whole = wet + mob * (rest * rest)
    inverse = pl.reciprocal(whole, approx=True)
    return wet * (inverse * (2.0 - whole * inverse))


def face(flux, below, here):
    return jnp.maximum(flux, 0.0) * below + jnp.minimum(flux, 0.0) * here


def columns_of(row):
    return jnp.transpose(jnp.broadcast_to(row, (LANES, row.shape[1])))


def kernel(
    tiles,
    members,
    sat_hbm,
    mob_hbm,
    pore_hbm,
    qx_hbm,
    qy_hbm,
    qz_hbm,
    cell_hbm,
    well_hbm,
    factor_hbm,
    obs_hbm,
    new_ref,
    parts,
    obs_all,
    sat,
    mob,
    pore,
    qx,
    qy,
    qz,
    cell_ref,
    well_ref,
    factor_ref,
    obs_ref,
    flow,
    beside,
    behind,
    sat_beside,
    sat_edge,
    fixed,
    q_below,
    q_above,
    partial,
    split,
    pick,
    lane_mask,
    well_mask,
    obs_line,
    in_sem,
    halo_send,
    halo_recv,
    obs_send,
    obs_recv,
    part_send,
    part_recv,
):
    tile = lax.axis_index("tile")
    member = lax.axis_index("member")
    rows, layers, columns = sat.shape
    last = rows - 1
    wells_dev = obs_ref.shape[1]
    wells = wells_dev * tiles
    conns = cell_ref.shape[1]
    has_lo = tile > 0
    has_hi = tile < tiles - 1

    barrier = pltpu.get_barrier_semaphore()

    def peer(dm, dt):
        to_member = member + dm
        to_tile = tile + dt
        return {
            "member": jnp.where(to_member >= members, to_member - members, to_member),
            "tile": jnp.where(to_tile >= tiles, to_tile - tiles, to_tile),
        }

    def for_peers(act):
        def far(dm, carry):
            for dt in range(tiles):
                act(dm, dt)
            return carry

        lax.fori_loop(1, members, far, 0)
        for dt in range(1, tiles):
            act(0, dt)

    def greet(dm, dt):
        pl.semaphore_signal(barrier, inc=1, device_id=peer(dm, dt), device_id_type=MESH)

    loads = [
        pltpu.make_async_copy(src, dst, in_sem.at[n])
        for n, (src, dst) in enumerate(
            (
                (sat_hbm.at[0, 0], sat.at[0]),
                (mob_hbm.at[0, 0], mob.at[0]),
                (sat_hbm.at[0, last], sat.at[last]),
                (mob_hbm.at[0, last], mob.at[last]),
                (sat_hbm.at[0, 1:last], sat.at[1:last]),
                (mob_hbm.at[0, 1:last], mob.at[1:last]),
                (qx_hbm.at[0], qx),
                (qz_hbm.at[0], qz),
                (qy_hbm.at[0], qy),
                (pore_hbm.at[0], pore),
                (obs_hbm, obs_ref),
                (cell_hbm, cell_ref),
                (well_hbm, well_ref),
                (factor_hbm, factor_ref),
            )
        )
    ]
    for load in loads[0:4]:
        load.start()
    for_peers(greet)
    for load in loads[4:]:
        load.start()


    def exchange(src, dst_at, peers, axis, me, send_sem, recv_sem):
        copies = []
        for d in range(1, peers):
            copies.append(
                pltpu.make_async_remote_copy(
                    src_ref=src,
                    dst_ref=dst_at,
                    send_sem=send_sem.at[d - 1],
                    recv_sem=recv_sem.at[d - 1],
                    device_id={axis: lax.rem(me + d, peers)},
                    device_id_type=MESH,
                )
            )
            copies[-1].start()
        return copies

    def to_side(n, up, src, dst):
        side = 0 if up else 1
        beyond = jnp.minimum(tile + 1, tiles - 1) if up else jnp.maximum(tile - 1, 0)
        return pltpu.make_async_remote_copy(
            src_ref=src,
            dst_ref=dst,
            send_sem=halo_send.at[side, n],
            recv_sem=halo_recv.at[side, n],
            device_id={"tile": beyond},
            device_id_type=MESH,
        )

    ups = [
        to_side(0, True, flow.at[0, last], beside.at[0]),
        to_side(1, True, qx_hbm.at[0, last], q_below),
    ]
    downs = [
        to_side(0, False, flow.at[0, 0], beside.at[1]),
        to_side(1, False, qx_hbm.at[0, 0:2], q_above),
    ]
    for n, field in enumerate((mob_hbm, pore_hbm, qz_hbm, qy_hbm)):
        ups.append(to_side(n + 2, True, field.at[0, last], fixed.at[0, n]))
        downs.append(to_side(n + 2, False, field.at[0, 0], fixed.at[1, n]))
    ups.append(to_side(6, True, flow.at[1, last - 1], behind.at[0]))
    downs.append(to_side(6, False, flow.at[1, 1], behind.at[1]))
    ups.append(to_side(7, True, sat_edge.at[1], sat_beside.at[0]))
    downs.append(to_side(7, False, sat_edge.at[0], sat_beside.at[1]))

    def send(start, stop):
        @pl.when(has_lo)
        def _():
            for copy in downs[start:stop]:
                copy.start()

        @pl.when(has_hi)
        def _():
            for copy in ups[start:stop]:
                copy.start()

    def receive(start, stop):
        @pl.when(has_lo)
        def _():
            for copy in ups[start:stop]:
                copy.wait_recv()

        @pl.when(has_hi)
        def _():
            for copy in downs[start:stop]:
                copy.wait_recv()

    def set_flow(k, i, value):
        flow[k, i] = value

    def set_split(k, i, value):
        high = value.astype(jnp.bfloat16)
        if isinstance(i, int):
            place = {0: 0, last: 1, 1: 2, last - 1: 3}[i]
        else:
            place = jnp.where(i == 1, 2, jnp.where(i == last - 1, 3, i + 2))
        at = pl.ds(pl.multiple_of(place * layers, layers), layers)
        split[k % 2, at, 0:columns] = high
        split[k % 2, at, columns : 2 * columns] = (value - high.astype(jnp.float32)).astype(jnp.bfloat16)

    for load in loads[0:4]:
        load.wait()
    set_flow(0, 0, frac(sat[0], mob[0]))
    set_flow(0, last, frac(sat[last], mob[last]))
    pl.semaphore_wait(barrier, tiles * members - 1)
    send(0, 6)

    loads[10].wait()
    obs_line[...] = jnp.zeros_like(obs_line)
    obs_line[0:SUBSTEPS, 0:wells_dev] = obs_ref[...]
    lines = [jnp.zeros((1, LANES), jnp.float32)] * parts.shape[2]
    for k in range(SUBSTEPS):
        row, lane = divmod(k * wells, LANES)
        lines[row] = lines[row] + pltpu.roll(
            obs_line[k : k + 1, :], lane + tile * wells_dev, 1
        )
    packed = jnp.concatenate(lines, axis=0)
    obs_all[tile] = jnp.where(packed == 0.0, 1.0, packed)
    obs_copies = exchange(obs_all.at[tile], obs_all.at[tile], tiles, "tile", tile, obs_send, obs_recv)

    def first_flow(i, carry):
        set_flow(0, i, frac(sat[i], mob[i]))
        return carry

    for load in loads[4:6]:
        load.wait()
    lax.fori_loop(1, last, first_flow, 0)
    for load in loads[6:10]:
        load.wait()

    col_ids = lax.broadcasted_iota(jnp.int32, (layers, columns), 1)
    lay_ids = lax.broadcasted_iota(jnp.int32, (layers, columns), 0)

    def spread_of(here, qz_i, qy_i):
        qz_i = jnp.where(lay_ids > 0, qz_i, 0.0)
        qy_i = jnp.where(col_ids > 0, qy_i, 0.0)
        face_z = face(qz_i, pltpu.roll(here, 1, 0), here)
        face_y = face(qy_i, pltpu.roll(here, 1, 1), here)
        return (pltpu.roll(face_z, layers - 1, 0) - face_z) + (
            pltpu.roll(face_y, columns - 1, 1) - face_y
        )

    def spread(k, i):
        return spread_of(flow[k, i], qz[i], qy[i])

    def face_at(k, i):
        return face(qx[i], flow[k, i - 1], flow[k, i])

    def store(k, i, after):
        if k + 1 < SUBSTEPS:
            sat[i] = after
        else:
            new_ref[0, i] = after
        value = frac(after, mob[i])
        set_flow(k + 1, i, value)
        return value

    def set_masks():
        for load in loads[11:]:
            load.wait()
        lane_ids = lax.broadcasted_iota(jnp.int32, (conns, LANES), 1)
        cell_col = columns_of(cell_ref[...])
        row_col = lax.shift_right_logical(cell_col, columns.bit_length() - 1)
        spot = jnp.where(row_col < layers, row_col, row_col + layers)
        spot = jnp.where(row_col < 2 * layers, spot, row_col + 2 * layers)
        spot = jnp.where(row_col < (last - 1) * layers, spot, row_col - (last - 4) * layers)
        spot = jnp.where(row_col < last * layers, spot, row_col - (last - 1) * layers)
        for b in range(rows * layers // LANES):
            pick[:, b * LANES : (b + 1) * LANES] = jnp.where(
                spot == lane_ids + b * LANES, 1.0, 0.0
            ).astype(jnp.bfloat16)
        lane_mask[...] = jnp.where(
            cell_col - row_col * columns == lane_ids, columns_of(factor_ref[...]), 0.0
        )
        well_mask[...] = jnp.where(columns_of(well_ref[...]) == lane_ids, 1.0, 0.0)

    step_rates = []
    two = 2 * layers
    four = 4 * layers
    cells = rows * layers

    def gather(k, start, stop):
        found = jnp.dot(
            pick[:, start:stop], split[k % 2, start:stop, :], preferred_element_type=jnp.float32
        )
        return found[:, 0:columns] + found[:, columns : 2 * columns]

    def add_rates(found):
        rate = jnp.sum(found * lane_mask[...], axis=1, keepdims=True) * well_mask[...]
        step_rates.append(jnp.sum(rate, axis=0, keepdims=True))

    def inner_rows(k, start, stop):
        def inner(i, face_lo):
            face_hi = face(qx[i + 1], flow[k, i], flow[k, i + 1])
            value = store(k, i, sat[i] - pore[i] * ((face_hi - face_lo) + spread(k, i)))
            set_split(k, i, value)
            return face_hi

        face_first = face_at(k, start)
        return face_first, lax.fori_loop(start, stop, inner, face_first)

    face_lo, face_hi = inner_rows(0, 1, last)
    send(6, 7)
    partial[0] = sat[0] - pore[0] * (face_lo + spread(0, 0))
    partial[1] = sat[last] - pore[last] * (spread(0, last) - face_hi)
    qx_first = jnp.where(has_lo, qx[0], 0.0)
    set_masks()
    found_first = gather(0, two, cells)
    receive(0, 2)

    @pl.when(jnp.logical_not(has_hi))
    def _():
        q_above[...] = jnp.zeros_like(q_above)

    below = jnp.where(has_lo, beside[0], 0.0)
    above = jnp.where(has_hi, beside[1], 0.0)
    first = partial[0] + pore[0] * face(qx_first, below, flow[0, 0])
    final = partial[1] - pore[last] * face(q_above[0], flow[0, last], above)
    sat_edge[0] = first
    sat_edge[1] = final
    send(7, 8)
    set_split(0, 0, store(0, 0, first))
    set_split(0, last, store(0, last, final))

    add_rates(found_first + gather(0, 0, two))
    face_lo, face_hi = inner_rows(1, 1, last)
    partial[0] = sat[0] - pore[0] * (face_lo + spread(1, 0))
    partial[1] = sat[last] - pore[last] * (spread(1, last) - face_hi)
    found_second = gather(1, two, cells)
    face_lo, face_hi = inner_rows(2, 2, last - 1)
    partial[2] = sat[1] - pore[1] * (face_lo + spread(2, 1))
    partial[3] = sat[last - 1] - pore[last - 1] * (spread(2, last - 1) - face_hi)
    found_third = gather(2, four, cells)
    receive(2, 8)

    def advance_beside(side, here, lower, upper):
        mob_i, pore_i, qz_i, qy_i = (fixed[side, n] for n in range(4))
        total = (upper - lower) + spread_of(here, qz_i, qy_i)
        return frac(sat_beside[side] - pore_i * total, mob_i)

    flow_lo = frac(sat_beside[0], fixed[0, 0])
    flow_hi = frac(sat_beside[1], fixed[1, 0])
    face_lo = face(qx_first, jnp.where(has_lo, flow_lo, 0.0), flow[1, 0])
    face_hi = face(q_above[0], flow[1, last], jnp.where(has_hi, flow_hi, 0.0))
    set_split(1, 0, store(1, 0, partial[0] + pore[0] * face_lo))
    set_split(1, last, store(1, last, partial[1] - pore[last] * face_hi))
    below = advance_beside(0, flow_lo, face(q_below[...], behind[0], flow_lo), face_lo)
    above = advance_beside(1, flow_hi, face_hi, face(q_above[1], flow_hi, behind[1]))

    face_lo = face(qx_first, jnp.where(has_lo, below, 0.0), flow[2, 0])
    face_hi = face(q_above[0], flow[2, last], jnp.where(has_hi, above, 0.0))
    face_one = face_at(2, 1)
    face_last = face_at(2, last)
    for i, after in (
        (0, sat[0] - pore[0] * ((face_one - face_lo) + spread(2, 0))),
        (1, partial[2] + pore[1] * face_one),
        (last - 1, partial[3] - pore[last - 1] * face_last),
        (last, sat[last] - pore[last] * ((face_hi - face_last) + spread(2, last))),
    ):
        set_split(2, i, store(2, i, after))
    add_rates(found_second + gather(1, 0, two))
    add_rates(found_third + gather(2, 0, four))

    lines = [jnp.zeros((1, LANES), jnp.float32)] * parts.shape[2]
    for k in range(SUBSTEPS):
        row, lane = divmod(k * wells, LANES)
        lines[row] = lines[row] + (pltpu.roll(step_rates[k], lane, 1) if lane else step_rates[k])
    parts[tile, member] = jnp.concatenate(lines, axis=0)

    def part_copy(dm, dt):
        n = dm * tiles + dt - 1
        return pltpu.make_async_remote_copy(
            src_ref=parts.at[tile, member],
            dst_ref=parts.at[tile, member],
            send_sem=part_send.at[n],
            recv_sem=part_recv.at[n],
            device_id=peer(dm, dt),
            device_id_type=MESH,
        )

    for_peers(lambda dm, dt: part_copy(dm, dt).start())
    for copy in obs_copies:
        copy.wait_recv()
    for_peers(lambda dm, dt: part_copy(dm, dt).wait_recv())

    @pl.when(has_lo)
    def _():
        for copy in downs:
            copy.wait_send()

    @pl.when(has_hi)
    def _():
        for copy in ups:
            copy.wait_send()

    for copy in obs_copies:
        copy.wait_send()
    for_peers(lambda dm, dt: part_copy(dm, dt).wait_send())


def finish(new_ref, parts, obs_all, new_hbm, rates_hbm, gram_hbm, rates, gram, out_sem):
    tile = lax.axis_index("tile")
    member = lax.axis_index("member")
    tiles, members = parts.shape[0:2]
    wells_dev = rates.shape[2]
    wells = wells_dev * tiles
    new_out = pltpu.make_async_copy(new_ref, new_hbm, out_sem.at[0])
    new_out.start()

    def tile_sum(m):
        whole = parts[0, m]
        for t in range(1, tiles):
            whole = whole + parts[t, m]
        return whole

    mine = tile_sum(member)
    for k in range(SUBSTEPS):
        row, lane = divmod(k * wells, LANES)
        moved = pltpu.roll(
            mine[row : row + 1], lax.rem(2 * LANES - lane - tile * wells_dev, LANES), 1
        )
        rates[k] = moved[:, 0:wells_dev]
    rates_out = pltpu.make_async_copy(rates, rates_hbm, out_sem.at[1])
    rates_out.start()
    obs = obs_all[0]
    for t in range(1, tiles):
        obs = obs * obs_all[t]
    data = [tile_sum(m) / obs for m in range(members)]
    mean = data[0]
    for m in range(1, members):
        mean = mean + data[m]
    mean = mean * (1.0 / members)
    own = mine / obs - mean
    terms = jnp.concatenate(
        [jnp.sum(own * (data[m] - mean), axis=0, keepdims=True) for m in range(members)], axis=0
    )
    terms = jnp.sum(terms, axis=1, keepdims=True)
    square = (members, LANES)
    diagonal = lax.broadcasted_iota(jnp.int32, square, 0) == lax.broadcasted_iota(
        jnp.int32, square, 1
    )
    line = jnp.sum(jnp.where(diagonal, terms, 0.0), axis=0, keepdims=True)
    gram[...] = line[:, 0:members] / (members - 1.0)
    gram_out = pltpu.make_async_copy(gram, gram_hbm, out_sem.at[2])
    gram_out.start()
    new_out.wait()
    rates_out.wait()
    gram_out.wait()


def body(tiles, members, sat, mob, pore, qx, qy, qz, cell, well, factor, obs):
    block = sat.shape[1:]
    rows, layers, columns = block
    conns = cell.shape[0]
    wells_dev = obs.shape[0]
    f32 = jnp.float32
    dma = pltpu.SemaphoreType.DMA
    hbm_spec = pl.BlockSpec(memory_space=pltpu.HBM)
    vmem_spec = pl.BlockSpec(memory_space=pltpu.VMEM)
    lines = -(-SUBSTEPS * wells_dev * tiles // LANES)
    new, parts, obs_all = pl.pallas_call(
        functools.partial(kernel, tiles, members),
        out_shape=(
            pltpu.VMEM(sat.shape, f32),
            pltpu.VMEM((tiles, members, lines, LANES), f32),
            pltpu.VMEM((tiles, lines, LANES), f32),
        ),
        in_specs=[hbm_spec] * 10,
        out_specs=(vmem_spec,) * 3,
        scratch_shapes=[pltpu.VMEM(block, f32)] * 6
        + [
            pltpu.VMEM((1, conns), jnp.int32),
            pltpu.VMEM((1, conns), jnp.int32),
            pltpu.VMEM((1, conns), f32),
            pltpu.VMEM((SUBSTEPS, wells_dev), f32),
            pltpu.VMEM((SUBSTEPS + 1,) + block, f32),
            pltpu.VMEM((2, layers, columns), f32),
            pltpu.VMEM((2, layers, columns), f32),
            pltpu.VMEM((2, layers, columns), f32),
            pltpu.VMEM((2, layers, columns), f32),
            pltpu.VMEM((2, 4, layers, columns), f32),
            pltpu.VMEM((layers, columns), f32),
            pltpu.VMEM((2, layers, columns), f32),
            pltpu.VMEM((4, layers, columns), f32),
            pltpu.VMEM((2, rows * layers, 2 * columns), jnp.bfloat16),
            pltpu.VMEM((conns, rows * layers), jnp.bfloat16),
            pltpu.VMEM((conns, LANES), f32),
            pltpu.VMEM((conns, LANES), f32),
            pltpu.VMEM((SUBLANES, LANES), f32),
            dma((14,)),
            dma((2, 8)),
            dma((2, 8)),
            dma((tiles - 1,)),
            dma((tiles - 1,)),
            dma((tiles * members - 1,)),
            dma((tiles * members - 1,)),
        ],
        compiler_params=pltpu.CompilerParams(
            collective_id=0, has_side_effects=True, vmem_limit_bytes=RUN_VMEM
        ),
        cost_estimate=pl.CostEstimate(
            flops=100 * SUBSTEPS * rows * layers * columns,
            bytes_accessed=28 * rows * layers * columns,
            transcendentals=0,
        ),
        name="transport",
    )(sat, mob, pore, qx, qy, qz, cell.reshape(1, -1), well.reshape(1, -1), factor.reshape(1, -1), obs.T)
    new, rates, gram = pl.pallas_call(
        finish,
        out_shape=(
            jax.ShapeDtypeStruct(sat.shape, f32),
            jax.ShapeDtypeStruct((SUBSTEPS, 1, wells_dev), f32),
            jax.ShapeDtypeStruct((1, members), f32),
        ),
        in_specs=[vmem_spec] * 3,
        out_specs=(hbm_spec,) * 3,
        scratch_shapes=[
            pltpu.VMEM((SUBSTEPS, 1, wells_dev), f32),
            pltpu.VMEM((1, members), f32),
            dma((3,)),
        ],
        compiler_params=pltpu.CompilerParams(vmem_limit_bytes=OUT_VMEM),
        name="finish",
    )(new, parts, obs_all)
    return new, jnp.transpose(rates, (1, 2, 0)), gram


def solution(mesh):
    field = P("member", "tile", None, None)
    in_specs = (field,) * 6 + (P("tile"), P("tile"), P("tile"), P("tile", None))
    out_specs = (field, P("member", "tile", None), P("member", None))
    run = functools.partial(body, mesh.shape["tile"], mesh.shape["member"])
    return jax.shard_map(run, mesh=mesh, in_specs=in_specs, out_specs=out_specs, check_vma=False)
```

```python
import functools

import jax
import jax.numpy as jnp
from jax import lax
from jax.experimental import pallas as pl
from jax.experimental.pallas import tpu as pltpu
from jax.sharding import PartitionSpec as P

SUBSTEPS = 3
LANES = 128
SUBLANES = 8
MESH = pl.DeviceIdType.MESH
RUN_VMEM = 60 * 1024 * 1024
OUT_VMEM = 4 * 1024 * 1024


def frac(sat, mob):
    wet = sat * sat
    rest = 1.0 - sat
    whole = wet + mob * (rest * rest)
    inverse = pl.reciprocal(whole, approx=True)
    return wet * (inverse * (2.0 - whole * inverse))


def face(flux, below, here):
    return jnp.maximum(flux, 0.0) * below + jnp.minimum(flux, 0.0) * here


def columns_of(row):
    return jnp.transpose(jnp.broadcast_to(row, (LANES, row.shape[1])))


def kernel(
    tiles,
    members,
    sat_hbm,
    mob_hbm,
    pore_hbm,
    qx_hbm,
    qy_hbm,
    qz_hbm,
    cell_hbm,
    well_hbm,
    factor_hbm,
    obs_hbm,
    new_ref,
    parts,
    obs_all,
    sat,
    mob,
    pore,
    qx,
    qy,
    qz,
    cell_ref,
    well_ref,
    factor_ref,
    obs_ref,
    flow,
    beside,
    behind,
    sat_beside,
    sat_edge,
    fixed,
    q_below,
    q_above,
    partial,
    split,
    pick,
    lane_mask,
    well_mask,
    obs_line,
    in_sem,
    halo_send,
    halo_recv,
    obs_send,
    obs_recv,
    part_send,
    part_recv,
):
    tile = lax.axis_index("tile")
    member = lax.axis_index("member")
    rows, layers, columns = sat.shape
    last = rows - 1
    wells_dev = obs_ref.shape[1]
    wells = wells_dev * tiles
    conns = cell_ref.shape[1]
    has_lo = tile > 0
    has_hi = tile < tiles - 1

    barrier = pltpu.get_barrier_semaphore()

    def peer(dm, dt):
        to_member = member + dm
        to_tile = tile + dt
        return {
            "member": jnp.where(to_member >= members, to_member - members, to_member),
            "tile": jnp.where(to_tile >= tiles, to_tile - tiles, to_tile),
        }

    def for_peers(act):
        def far(dm, carry):
            for dt in range(tiles):
                act(dm, dt)
            return carry

        lax.fori_loop(1, members, far, 0)
        for dt in range(1, tiles):
            act(0, dt)

    def greet(dm, dt):
        pl.semaphore_signal(barrier, inc=1, device_id=peer(dm, dt), device_id_type=MESH)

    loads = [
        pltpu.make_async_copy(src, dst, in_sem.at[n])
        for n, (src, dst) in enumerate(
            (
                (sat_hbm.at[0, 0], sat.at[0]),
                (mob_hbm.at[0, 0], mob.at[0]),
                (sat_hbm.at[0, last], sat.at[last]),
                (mob_hbm.at[0, last], mob.at[last]),
                (sat_hbm.at[0, 1:last], sat.at[1:last]),
                (mob_hbm.at[0, 1:last], mob.at[1:last]),
                (qx_hbm.at[0], qx),
                (qz_hbm.at[0], qz),
                (qy_hbm.at[0], qy),
                (pore_hbm.at[0], pore),
                (obs_hbm, obs_ref),
                (cell_hbm, cell_ref),
                (well_hbm, well_ref),
                (factor_hbm, factor_ref),
            )
        )
    ]
    for load in loads[0:4]:
        load.start()
    for_peers(greet)
    for load in loads[4:]:
        load.start()

    def exchange(src, dst_at, peers, axis, me, send_sem, recv_sem):
        copies = []
        for d in range(1, peers):
            copies.append(
                pltpu.make_async_remote_copy(
                    src_ref=src,
                    dst_ref=dst_at,
                    send_sem=send_sem.at[d - 1],
                    recv_sem=recv_sem.at[d - 1],
                    device_id={axis: lax.rem(me + d, peers)},
                    device_id_type=MESH,
                )
            )
            copies[-1].start()
        return copies

    def to_side(n, up, src, dst):
        side = 0 if up else 1
        beyond = jnp.minimum(tile + 1, tiles - 1) if up else jnp.maximum(tile - 1, 0)
        return pltpu.make_async_remote_copy(
            src_ref=src,
            dst_ref=dst,
            send_sem=halo_send.at[side, n],
            recv_sem=halo_recv.at[side, n],
            device_id={"tile": beyond},
            device_id_type=MESH,
        )

    ups = [
        to_side(0, True, flow.at[0, last], beside.at[0]),
        to_side(1, True, qx_hbm.at[0, last], q_below),
    ]
    downs = [
        to_side(0, False, flow.at[0, 0], beside.at[1]),
        to_side(1, False, qx_hbm.at[0, 0:2], q_above),
    ]
    for n, field in enumerate((mob_hbm, pore_hbm, qz_hbm, qy_hbm)):
        ups.append(to_side(n + 2, True, field.at[0, last], fixed.at[0, n]))
        downs.append(to_side(n + 2, False, field.at[0, 0], fixed.at[1, n]))
    ups.append(to_side(6, True, flow.at[1, last - 1], behind.at[0]))
    downs.append(to_side(6, False, flow.at[1, 1], behind.at[1]))
    ups.append(to_side(7, True, sat_edge.at[1], sat_beside.at[0]))
    downs.append(to_side(7, False, sat_edge.at[0], sat_beside.at[1]))

    def send(start, stop):
        @pl.when(has_lo)
        def _():
            for copy in downs[start:stop]:
                copy.start()

        @pl.when(has_hi)
        def _():
            for copy in ups[start:stop]:
                copy.start()

    def receive(start, stop):
        @pl.when(has_lo)
        def _():
            for copy in ups[start:stop]:
                copy.wait_recv()

        @pl.when(has_hi)
        def _():
            for copy in downs[start:stop]:
                copy.wait_recv()

    def set_flow(k, i, value):
        flow[k, i] = value

    def set_split(k, i, value):
        high = value.astype(jnp.bfloat16)
        if isinstance(i, int):
            place = {0: 0, last: 1, 1: 2, last - 1: 3}[i]
        else:
            place = jnp.where(i == 1, 2, jnp.where(i == last - 1, 3, i + 2))
        at = pl.ds(pl.multiple_of(place * layers, layers), layers)
        split[k % 2, at, 0:columns] = high
        split[k % 2, at, columns : 2 * columns] = (value - high.astype(jnp.float32)).astype(jnp.bfloat16)

    for load in loads[0:4]:
        load.wait()
    set_flow(0, 0, frac(sat[0], mob[0]))
    set_flow(0, last, frac(sat[last], mob[last]))
    pl.semaphore_wait(barrier, tiles * members - 1)
    send(0, 1)
    send(1, 2)

    def first_flow(i, carry):
        set_flow(0, i, frac(sat[i], mob[i]))
        return carry

    for load in loads[4:6]:
        load.wait()
    lax.fori_loop(1, last, first_flow, 0)
    send(2, 6)
    loads[10].wait()
    obs_line[...] = jnp.zeros_like(obs_line)
    obs_line[0:SUBSTEPS, 0:wells_dev] = obs_ref[...]
    lines = [jnp.zeros((1, LANES), jnp.float32)] * parts.shape[2]
    for k in range(SUBSTEPS):
        row, lane = divmod(k * wells, LANES)
        lines[row] = lines[row] + pltpu.roll(
            obs_line[k : k + 1, :], lane + tile * wells_dev, 1
        )
    packed = jnp.concatenate(lines, axis=0)
    obs_all[tile] = jnp.where(packed == 0.0, 1.0, packed)
    obs_copies = exchange(obs_all.at[tile], obs_all.at[tile], tiles, "tile", tile, obs_send, obs_recv)
    for load in loads[6:10]:
        load.wait()

    col_ids = lax.broadcasted_iota(jnp.int32, (layers, columns), 1)
    lay_ids = lax.broadcasted_iota(jnp.int32, (layers, columns), 0)

    def spread_of(here, qz_i, qy_i):
        qz_i = jnp.where(lay_ids > 0, qz_i, 0.0)
        qy_i = jnp.where(col_ids > 0, qy_i, 0.0)
        face_z = face(qz_i, pltpu.roll(here, 1, 0), here)
        face_y = face(qy_i, pltpu.roll(here, 1, 1), here)
        return (pltpu.roll(face_z, layers - 1, 0) - face_z) + (
            pltpu.roll(face_y, columns - 1, 1) - face_y
        )

    def spread(k, i):
        return spread_of(flow[k, i], qz[i], qy[i])

    def face_at(k, i):
        return face(qx[i], flow[k, i - 1], flow[k, i])

    def store(k, i, after):
        if k + 1 < SUBSTEPS:
            sat[i] = after
        else:
            new_ref[0, i] = after
        value = frac(after, mob[i])
        set_flow(k + 1, i, value)
        return value

    def set_masks():
        for load in loads[11:]:
            load.wait()
        lane_ids = lax.broadcasted_iota(jnp.int32, (conns, LANES), 1)
        cell_col = columns_of(cell_ref[...])
        row_col = lax.shift_right_logical(cell_col, columns.bit_length() - 1)
        spot = jnp.where(row_col < layers, row_col, row_col + layers)
        spot = jnp.where(row_col < 2 * layers, spot, row_col + 2 * layers)
        spot = jnp.where(row_col < (last - 1) * layers, spot, row_col - (last - 4) * layers)
        spot = jnp.where(row_col < last * layers, spot, row_col - (last - 1) * layers)
        for b in range(rows * layers // LANES):
            pick[:, b * LANES : (b + 1) * LANES] = jnp.where(
                spot == lane_ids + b * LANES, 1.0, 0.0
            ).astype(jnp.bfloat16)
        lane_mask[...] = jnp.where(
            cell_col - row_col * columns == lane_ids, columns_of(factor_ref[...]), 0.0
        )
        well_mask[...] = jnp.where(columns_of(well_ref[...]) == lane_ids, 1.0, 0.0)

    step_rates = []
    two = 2 * layers
    four = 4 * layers
    cells = rows * layers

    def gather(k, start, stop):
        found = jnp.dot(
            pick[:, start:stop], split[k % 2, start:stop, :], preferred_element_type=jnp.float32
        )
        return found[:, 0:columns] + found[:, columns : 2 * columns]

    def add_rates(found):
        rate = jnp.sum(found * lane_mask[...], axis=1, keepdims=True) * well_mask[...]
        step_rates.append(jnp.sum(rate, axis=0, keepdims=True))

    def inner_rows(k, start, stop):
        def inner(i, face_lo):
            face_hi = face(qx[i + 1], flow[k, i], flow[k, i + 1])
            value = store(k, i, sat[i] - pore[i] * ((face_hi - face_lo) + spread(k, i)))
            set_split(k, i, value)
            return face_hi

        face_first = face_at(k, start)
        return face_first, lax.fori_loop(start, stop, inner, face_first)

    face_lo, face_hi = inner_rows(0, 1, last)
    send(6, 7)
    partial[0] = sat[0] - pore[0] * (face_lo + spread(0, 0))
    partial[1] = sat[last] - pore[last] * (spread(0, last) - face_hi)
    qx_first = jnp.where(has_lo, qx[0], 0.0)
    set_masks()
    found_first = gather(0, two, cells)
    receive(0, 2)

    @pl.when(jnp.logical_not(has_hi))
    def _():
        q_above[...] = jnp.zeros_like(q_above)

    below = jnp.where(has_lo, beside[0], 0.0)
    above = jnp.where(has_hi, beside[1], 0.0)
    first = partial[0] + pore[0] * face(qx_first, below, flow[0, 0])
    final = partial[1] - pore[last] * face(q_above[0], flow[0, last], above)
    sat_edge[0] = first
    sat_edge[1] = final
    send(7, 8)
    set_split(0, 0, store(0, 0, first))
    set_split(0, last, store(0, last, final))

    add_rates(found_first + gather(0, 0, two))
    face_lo, face_hi = inner_rows(1, 1, last)
    partial[0] = sat[0] - pore[0] * (face_lo + spread(1, 0))
    partial[1] = sat[last] - pore[last] * (spread(1, last) - face_hi)
    found_second = gather(1, two, cells)
    face_lo, face_hi = inner_rows(2, 2, last - 1)
    partial[2] = sat[1] - pore[1] * (face_lo + spread(2, 1))
    partial[3] = sat[last - 1] - pore[last - 1] * (spread(2, last - 1) - face_hi)
    found_third = gather(2, four, cells)
    receive(2, 8)

    def advance_beside(side, here, lower, upper):
        mob_i, pore_i, qz_i, qy_i = (fixed[side, n] for n in range(4))
        total = (upper - lower) + spread_of(here, qz_i, qy_i)
        return frac(sat_beside[side] - pore_i * total, mob_i)

    flow_lo = frac(sat_beside[0], fixed[0, 0])
    flow_hi = frac(sat_beside[1], fixed[1, 0])
    face_lo = face(qx_first, jnp.where(has_lo, flow_lo, 0.0), flow[1, 0])
    face_hi = face(q_above[0], flow[1, last], jnp.where(has_hi, flow_hi, 0.0))
    set_split(1, 0, store(1, 0, partial[0] + pore[0] * face_lo))
    set_split(1, last, store(1, last, partial[1] - pore[last] * face_hi))
    below = advance_beside(0, flow_lo, face(q_below[...], behind[0], flow_lo), face_lo)
    above = advance_beside(1, flow_hi, face_hi, face(q_above[1], flow_hi, behind[1]))

    face_lo = face(qx_first, jnp.where(has_lo, below, 0.0), flow[2, 0])
    face_hi = face(q_above[0], flow[2, last], jnp.where(has_hi, above, 0.0))
    face_one = face_at(2, 1)
    face_last = face_at(2, last)
    for i, after in (
        (0, sat[0] - pore[0] * ((face_one - face_lo) + spread(2, 0))),
        (1, partial[2] + pore[1] * face_one),
        (last - 1, partial[3] - pore[last - 1] * face_last),
        (last, sat[last] - pore[last] * ((face_hi - face_last) + spread(2, last))),
    ):
        set_split(2, i, store(2, i, after))
    add_rates(found_second + gather(1, 0, two))
    add_rates(found_third + gather(2, 0, four))

    lines = [jnp.zeros((1, LANES), jnp.float32)] * parts.shape[2]
    for k in range(SUBSTEPS):
        row, lane = divmod(k * wells, LANES)
        lines[row] = lines[row] + (pltpu.roll(step_rates[k], lane, 1) if lane else step_rates[k])
    parts[tile, member] = jnp.concatenate(lines, axis=0)

    def part_copy(dm, dt):
        n = dm * tiles + dt - 1
        return pltpu.make_async_remote_copy(
            src_ref=parts.at[tile, member],
            dst_ref=parts.at[tile, member],
            send_sem=part_send.at[n],
            recv_sem=part_recv.at[n],
            device_id=peer(dm, dt),
            device_id_type=MESH,
        )

    for_peers(lambda dm, dt: part_copy(dm, dt).start())
    for copy in obs_copies:
        copy.wait_recv()
    for_peers(lambda dm, dt: part_copy(dm, dt).wait_recv())

    @pl.when(has_lo)
    def _():
        for copy in downs:
            copy.wait_send()

    @pl.when(has_hi)
    def _():
        for copy in ups:
            copy.wait_send()

    for copy in obs_copies:
        copy.wait_send()
    for_peers(lambda dm, dt: part_copy(dm, dt).wait_send())


def finish(new_ref, parts, obs_all, new_hbm, rates_hbm, gram_hbm, rates, gram, out_sem):
    tile = lax.axis_index("tile")
    member = lax.axis_index("member")
    tiles, members = parts.shape[0:2]
    wells_dev = rates.shape[2]
    wells = wells_dev * tiles
    new_out = pltpu.make_async_copy(new_ref, new_hbm, out_sem.at[0])
    new_out.start()

    def tile_sum(m):
        whole = parts[0, m]
        for t in range(1, tiles):
            whole = whole + parts[t, m]
        return whole

    mine = tile_sum(member)
    for k in range(SUBSTEPS):
        row, lane = divmod(k * wells, LANES)
        moved = pltpu.roll(
            mine[row : row + 1], lax.rem(2 * LANES - lane - tile * wells_dev, LANES), 1
        )
        rates[k] = moved[:, 0:wells_dev]
    rates_out = pltpu.make_async_copy(rates, rates_hbm, out_sem.at[1])
    rates_out.start()
    obs = obs_all[0]
    for t in range(1, tiles):
        obs = obs * obs_all[t]
    data = [tile_sum(m) / obs for m in range(members)]
    mean = data[0]
    for m in range(1, members):
        mean = mean + data[m]
    mean = mean * (1.0 / members)
    own = mine / obs - mean
    terms = jnp.concatenate(
        [jnp.sum(own * (data[m] - mean), axis=0, keepdims=True) for m in range(members)], axis=0
    )
    terms = jnp.sum(terms, axis=1, keepdims=True)
    square = (members, LANES)
    diagonal = lax.broadcasted_iota(jnp.int32, square, 0) == lax.broadcasted_iota(
        jnp.int32, square, 1
    )
    line = jnp.sum(jnp.where(diagonal, terms, 0.0), axis=0, keepdims=True)
    gram[...] = line[:, 0:members] / (members - 1.0)
    gram_out = pltpu.make_async_copy(gram, gram_hbm, out_sem.at[2])
    gram_out.start()
    new_out.wait()
    rates_out.wait()
    gram_out.wait()


def body(tiles, members, sat, mob, pore, qx, qy, qz, cell, well, factor, obs):
    block = sat.shape[1:]
    rows, layers, columns = block
    conns = cell.shape[0]
    wells_dev = obs.shape[0]
    f32 = jnp.float32
    dma = pltpu.SemaphoreType.DMA
    hbm_spec = pl.BlockSpec(memory_space=pltpu.HBM)
    vmem_spec = pl.BlockSpec(memory_space=pltpu.VMEM)
    lines = -(-SUBSTEPS * wells_dev * tiles // LANES)
    new, parts, obs_all = pl.pallas_call(
        functools.partial(kernel, tiles, members),
        out_shape=(
            pltpu.VMEM(sat.shape, f32),
            pltpu.VMEM((tiles, members, lines, LANES), f32),
            pltpu.VMEM((tiles, lines, LANES), f32),
        ),
        in_specs=[hbm_spec] * 10,
        out_specs=(vmem_spec,) * 3,
        scratch_shapes=[pltpu.VMEM(block, f32)] * 6
        + [
            pltpu.VMEM((1, conns), jnp.int32),
            pltpu.VMEM((1, conns), jnp.int32),
            pltpu.VMEM((1, conns), f32),
            pltpu.VMEM((SUBSTEPS, wells_dev), f32),
            pltpu.VMEM((SUBSTEPS + 1,) + block, f32),
            pltpu.VMEM((2, layers, columns), f32),
            pltpu.VMEM((2, layers, columns), f32),
            pltpu.VMEM((2, layers, columns), f32),
            pltpu.VMEM((2, layers, columns), f32),
            pltpu.VMEM((2, 4, layers, columns), f32),
            pltpu.VMEM((layers, columns), f32),
            pltpu.VMEM((2, layers, columns), f32),
            pltpu.VMEM((4, layers, columns), f32),
            pltpu.VMEM((2, rows * layers, 2 * columns), jnp.bfloat16),
            pltpu.VMEM((conns, rows * layers), jnp.bfloat16),
            pltpu.VMEM((conns, LANES), f32),
            pltpu.VMEM((conns, LANES), f32),
            pltpu.VMEM((SUBLANES, LANES), f32),
            dma((14,)),
            dma((2, 8)),
            dma((2, 8)),
            dma((tiles - 1,)),
            dma((tiles - 1,)),
            dma((tiles * members - 1,)),
            dma((tiles * members - 1,)),
        ],
        compiler_params=pltpu.CompilerParams(
            collective_id=0, has_side_effects=True, vmem_limit_bytes=RUN_VMEM
        ),
        cost_estimate=pl.CostEstimate(
            flops=100 * SUBSTEPS * rows * layers * columns,
            bytes_accessed=28 * rows * layers * columns,
            transcendentals=0,
        ),
        name="transport",
    )(sat, mob, pore, qx, qy, qz, cell.reshape(1, -1), well.reshape(1, -1), factor.reshape(1, -1), obs.T)
    new, rates, gram = pl.pallas_call(
        finish,
        out_shape=(
            jax.ShapeDtypeStruct(sat.shape, f32),
            jax.ShapeDtypeStruct((SUBSTEPS, 1, wells_dev), f32),
            jax.ShapeDtypeStruct((1, members), f32),
        ),
        in_specs=[vmem_spec] * 3,
        out_specs=(hbm_spec,) * 3,
        scratch_shapes=[
            pltpu.VMEM((SUBSTEPS, 1, wells_dev), f32),
            pltpu.VMEM((1, members), f32),
            dma((3,)),
        ],
        compiler_params=pltpu.CompilerParams(vmem_limit_bytes=OUT_VMEM),
        name="finish",
    )(new, parts, obs_all)
    return new, jnp.transpose(rates, (1, 2, 0)), gram


def solution(mesh):
    field = P("member", "tile", None, None)
    in_specs = (field,) * 6 + (P("tile"), P("tile"), P("tile"), P("tile", None))
    out_specs = (field, P("member", "tile", None), P("member", None))
    run = functools.partial(body, mesh.shape["tile"], mesh.shape["member"])
    return jax.shard_map(run, mesh=mesh, in_specs=in_specs, out_specs=out_specs, check_vma=False)
```

```python
import functools

import jax
import jax.numpy as jnp
from jax import lax
from jax.experimental import pallas as pl
from jax.experimental.pallas import tpu as pltpu
from jax.sharding import PartitionSpec as P

SUBSTEPS = 3
LANES = 128
SUBLANES = 8
MESH = pl.DeviceIdType.MESH
RUN_VMEM = 60 * 1024 * 1024
OUT_VMEM = 4 * 1024 * 1024


def frac(sat, mob):
    wet = sat * sat
    rest = 1.0 - sat
    whole = wet + mob * (rest * rest)
    inverse = pl.reciprocal(whole, approx=True)
    return wet * (inverse * (2.0 - whole * inverse))


def face(flux, below, here):
    return jnp.maximum(flux, 0.0) * below + jnp.minimum(flux, 0.0) * here


def columns_of(row):
    return jnp.transpose(jnp.broadcast_to(row, (LANES, row.shape[1])))


def kernel(
    tiles,
    members,
    sat_hbm,
    mob_hbm,
    pore_hbm,
    qx_hbm,
    qy_hbm,
    qz_hbm,
    cell_hbm,
    well_hbm,
    factor_hbm,
    obs_hbm,
    new_ref,
    parts,
    obs_all,
    sat,
    mob,
    pore,
    qx,
    qy,
    qz,
    cell_ref,
    well_ref,
    factor_ref,
    obs_ref,
    flow,
    beside,
    behind,
    sat_beside,
    sat_edge,
    fixed,
    q_below,
    q_above,
    partial,
    split,
    pick,
    lane_mask,
    well_mask,
    obs_line,
    in_sem,
    halo_send,
    halo_recv,
    obs_send,
    obs_recv,
    part_send,
    part_recv,
):
    tile = lax.axis_index("tile")
    member = lax.axis_index("member")
    rows, layers, columns = sat.shape
    last = rows - 1
    wells_dev = obs_ref.shape[1]
    wells = wells_dev * tiles
    conns = cell_ref.shape[1]
    has_lo = tile > 0
    has_hi = tile < tiles - 1

    barrier = pltpu.get_barrier_semaphore()

    def peer(dm, dt):
        to_member = member + dm
        to_tile = tile + dt
        return {
            "member": jnp.where(to_member >= members, to_member - members, to_member),
            "tile": jnp.where(to_tile >= tiles, to_tile - tiles, to_tile),
        }

    def for_peers(act):
        def far(dm, carry):
            for dt in range(tiles):
                act(dm, dt)
            return carry

        lax.fori_loop(1, members, far, 0)
        for dt in range(1, tiles):
            act(0, dt)

    def greet(dm, dt):
        pl.semaphore_signal(barrier, inc=1, device_id=peer(dm, dt), device_id_type=MESH)

    loads = [
        pltpu.make_async_copy(src, dst, in_sem.at[n])
        for n, (src, dst) in enumerate(
            (
                (sat_hbm.at[0, 0], sat.at[0]),
                (mob_hbm.at[0, 0], mob.at[0]),
                (sat_hbm.at[0, last], sat.at[last]),
                (mob_hbm.at[0, last], mob.at[last]),
                (sat_hbm.at[0, 1:last], sat.at[1:last]),
                (mob_hbm.at[0, 1:last], mob.at[1:last]),
                (qx_hbm.at[0], qx),
                (qz_hbm.at[0], qz),
                (qy_hbm.at[0], qy),
                (pore_hbm.at[0], pore),
                (obs_hbm, obs_ref),
                (cell_hbm, cell_ref),
                (well_hbm, well_ref),
                (factor_hbm, factor_ref),
            )
        )
    ]
    for load in loads[0:4]:
        load.start()
    for_peers(greet)
    for load in loads[4:]:
        load.start()

    def exchange(src, dst_at, peers, axis, me, send_sem, recv_sem):
        copies = []
        for d in range(1, peers):
            copies.append(
                pltpu.make_async_remote_copy(
                    src_ref=src,
                    dst_ref=dst_at,
                    send_sem=send_sem.at[d - 1],
                    recv_sem=recv_sem.at[d - 1],
                    device_id={axis: lax.rem(me + d, peers)},
                    device_id_type=MESH,
                )
            )
            copies[-1].start()
        return copies

    def to_side(n, up, src, dst):
        side = 0 if up else 1
        beyond = jnp.minimum(tile + 1, tiles - 1) if up else jnp.maximum(tile - 1, 0)
        return pltpu.make_async_remote_copy(
            src_ref=src,
            dst_ref=dst,
            send_sem=halo_send.at[side, n],
            recv_sem=halo_recv.at[side, n],
            device_id={"tile": beyond},
            device_id_type=MESH,
        )

    ups = [
        to_side(0, True, flow.at[0, last], beside.at[0]),
        to_side(1, True, qx_hbm.at[0, last], q_below),
    ]
    downs = [
        to_side(0, False, flow.at[0, 0], beside.at[1]),
        to_side(1, False, qx_hbm.at[0, 0:2], q_above),
    ]
    for n, field in enumerate((mob_hbm, pore_hbm, qz_hbm, qy_hbm)):
        ups.append(to_side(n + 2, True, field.at[0, last], fixed.at[0, n]))
        downs.append(to_side(n + 2, False, field.at[0, 0], fixed.at[1, n]))
    ups.append(to_side(6, True, flow.at[1, last - 1], behind.at[0]))
    downs.append(to_side(6, False, flow.at[1, 1], behind.at[1]))
    ups.append(to_side(7, True, sat_edge.at[1], sat_beside.at[0]))
    downs.append(to_side(7, False, sat_edge.at[0], sat_beside.at[1]))

    def send(start, stop):
        @pl.when(has_lo)
        def _():
            for copy in downs[start:stop]:
                copy.start()

        @pl.when(has_hi)
        def _():
            for copy in ups[start:stop]:
                copy.start()

    def receive(start, stop):
        @pl.when(has_lo)
        def _():
            for copy in ups[start:stop]:
                copy.wait_recv()

        @pl.when(has_hi)
        def _():
            for copy in downs[start:stop]:
                copy.wait_recv()

    def set_flow(k, i, value):
        flow[k, i] = value

    def set_split(k, i, value):
        high = value.astype(jnp.bfloat16)
        if isinstance(i, int):
            place = {0: 0, last: 1, 1: 2, last - 1: 3}[i]
        else:
            place = jnp.where(i == 1, 2, jnp.where(i == last - 1, 3, i + 2))
        at = pl.ds(pl.multiple_of(place * layers, layers), layers)
        split[k % 2, at, 0:columns] = high
        split[k % 2, at, columns : 2 * columns] = (value - high.astype(jnp.float32)).astype(jnp.bfloat16)

    for load in loads[0:4]:
        load.wait()
    set_flow(0, 0, frac(sat[0], mob[0]))
    set_flow(0, last, frac(sat[last], mob[last]))
    def set_masks():
        for load in loads[11:]:
            load.wait()
        lane_ids = lax.broadcasted_iota(jnp.int32, (conns, LANES), 1)
        cell_col = columns_of(cell_ref[...])
        row_col = lax.shift_right_logical(cell_col, columns.bit_length() - 1)
        spot = jnp.where(row_col < layers, row_col, row_col + layers)
        spot = jnp.where(row_col < 2 * layers, spot, row_col + 2 * layers)
        spot = jnp.where(row_col < (last - 1) * layers, spot, row_col - (last - 4) * layers)
        spot = jnp.where(row_col < last * layers, spot, row_col - (last - 1) * layers)
        for b in range(rows * layers // LANES):
            pick[:, b * LANES : (b + 1) * LANES] = jnp.where(
                spot == lane_ids + b * LANES, 1.0, 0.0
            ).astype(jnp.bfloat16)
        lane_mask[...] = jnp.where(
            cell_col - row_col * columns == lane_ids, columns_of(factor_ref[...]), 0.0
        )
        well_mask[...] = jnp.where(columns_of(well_ref[...]) == lane_ids, 1.0, 0.0)

    set_masks()
    pl.semaphore_wait(barrier, tiles * members - 1)
    send(0, 6)

    loads[10].wait()
    obs_line[...] = jnp.zeros_like(obs_line)
    obs_line[0:SUBSTEPS, 0:wells_dev] = obs_ref[...]
    lines = [jnp.zeros((1, LANES), jnp.float32)] * parts.shape[2]
    for k in range(SUBSTEPS):
        row, lane = divmod(k * wells, LANES)
        lines[row] = lines[row] + pltpu.roll(
            obs_line[k : k + 1, :], lane + tile * wells_dev, 1
        )
    packed = jnp.concatenate(lines, axis=0)
    obs_all[tile] = jnp.where(packed == 0.0, 1.0, packed)
    obs_copies = exchange(obs_all.at[tile], obs_all.at[tile], tiles, "tile", tile, obs_send, obs_recv)

    def first_flow(i, carry):
        set_flow(0, i, frac(sat[i], mob[i]))
        return carry

    for load in loads[4:6]:
        load.wait()
    lax.fori_loop(1, last, first_flow, 0)
    for load in loads[6:10]:
        load.wait()

    col_ids = lax.broadcasted_iota(jnp.int32, (layers, columns), 1)
    lay_ids = lax.broadcasted_iota(jnp.int32, (layers, columns), 0)

    def spread_of(here, qz_i, qy_i):
        qz_i = jnp.where(lay_ids > 0, qz_i, 0.0)
        qy_i = jnp.where(col_ids > 0, qy_i, 0.0)
        face_z = face(qz_i, pltpu.roll(here, 1, 0), here)
        face_y = face(qy_i, pltpu.roll(here, 1, 1), here)
        return (pltpu.roll(face_z, layers - 1, 0) - face_z) + (
            pltpu.roll(face_y, columns - 1, 1) - face_y
        )

    def spread(k, i):
        return spread_of(flow[k, i], qz[i], qy[i])

    def face_at(k, i):
        return face(qx[i], flow[k, i - 1], flow[k, i])

    def store(k, i, after):
        if k + 1 < SUBSTEPS:
            sat[i] = after
        else:
            new_ref[0, i] = after
        value = frac(after, mob[i])
        set_flow(k + 1, i, value)
        return value

    step_rates = []
    two = 2 * layers
    four = 4 * layers
    cells = rows * layers

    def gather(k, start, stop):
        found = jnp.dot(
            pick[:, start:stop], split[k % 2, start:stop, :], preferred_element_type=jnp.float32
        )
        return found[:, 0:columns] + found[:, columns : 2 * columns]

    def add_rates(found):
        rate = jnp.sum(found * lane_mask[...], axis=1, keepdims=True) * well_mask[...]
        step_rates.append(jnp.sum(rate, axis=0, keepdims=True))

    def inner_rows(k, start, stop):
        def inner(i, face_lo):
            face_hi = face(qx[i + 1], flow[k, i], flow[k, i + 1])
            value = store(k, i, sat[i] - pore[i] * ((face_hi - face_lo) + spread(k, i)))
            set_split(k, i, value)
            return face_hi

        face_first = face_at(k, start)
        return face_first, lax.fori_loop(start, stop, inner, face_first)

    face_lo, face_hi = inner_rows(0, 1, last)
    send(6, 7)
    partial[0] = sat[0] - pore[0] * (face_lo + spread(0, 0))
    partial[1] = sat[last] - pore[last] * (spread(0, last) - face_hi)
    qx_first = jnp.where(has_lo, qx[0], 0.0)
    found_first = gather(0, two, cells)
    receive(0, 2)

    @pl.when(jnp.logical_not(has_hi))
    def _():
        q_above[...] = jnp.zeros_like(q_above)

    below = jnp.where(has_lo, beside[0], 0.0)
    above = jnp.where(has_hi, beside[1], 0.0)
    first = partial[0] + pore[0] * face(qx_first, below, flow[0, 0])
    final = partial[1] - pore[last] * face(q_above[0], flow[0, last], above)
    sat_edge[0] = first
    sat_edge[1] = final
    send(7, 8)
    set_split(0, 0, store(0, 0, first))
    set_split(0, last, store(0, last, final))

    add_rates(found_first + gather(0, 0, two))
    face_lo, face_hi = inner_rows(1, 1, last)
    partial[0] = sat[0] - pore[0] * (face_lo + spread(1, 0))
    partial[1] = sat[last] - pore[last] * (spread(1, last) - face_hi)
    found_second = gather(1, two, cells)
    face_lo, face_hi = inner_rows(2, 2, last - 1)
    partial[2] = sat[1] - pore[1] * (face_lo + spread(2, 1))
    partial[3] = sat[last - 1] - pore[last - 1] * (spread(2, last - 1) - face_hi)
    found_third = gather(2, four, cells)
    receive(2, 8)

    def advance_beside(side, here, lower, upper):
        mob_i, pore_i, qz_i, qy_i = (fixed[side, n] for n in range(4))
        total = (upper - lower) + spread_of(here, qz_i, qy_i)
        return frac(sat_beside[side] - pore_i * total, mob_i)

    flow_lo = frac(sat_beside[0], fixed[0, 0])
    flow_hi = frac(sat_beside[1], fixed[1, 0])
    face_lo = face(qx_first, jnp.where(has_lo, flow_lo, 0.0), flow[1, 0])
    face_hi = face(q_above[0], flow[1, last], jnp.where(has_hi, flow_hi, 0.0))
    set_split(1, 0, store(1, 0, partial[0] + pore[0] * face_lo))
    set_split(1, last, store(1, last, partial[1] - pore[last] * face_hi))
    below = advance_beside(0, flow_lo, face(q_below[...], behind[0], flow_lo), face_lo)
    above = advance_beside(1, flow_hi, face_hi, face(q_above[1], flow_hi, behind[1]))

    face_lo = face(qx_first, jnp.where(has_lo, below, 0.0), flow[2, 0])
    face_hi = face(q_above[0], flow[2, last], jnp.where(has_hi, above, 0.0))
    face_one = face_at(2, 1)
    face_last = face_at(2, last)
    for i, after in (
        (0, sat[0] - pore[0] * ((face_one - face_lo) + spread(2, 0))),
        (1, partial[2] + pore[1] * face_one),
        (last - 1, partial[3] - pore[last - 1] * face_last),
        (last, sat[last] - pore[last] * ((face_hi - face_last) + spread(2, last))),
    ):
        set_split(2, i, store(2, i, after))
    add_rates(found_second + gather(1, 0, two))
    add_rates(found_third + gather(2, 0, four))

    lines = [jnp.zeros((1, LANES), jnp.float32)] * parts.shape[2]
    for k in range(SUBSTEPS):
        row, lane = divmod(k * wells, LANES)
        lines[row] = lines[row] + (pltpu.roll(step_rates[k], lane, 1) if lane else step_rates[k])
    parts[tile, member] = jnp.concatenate(lines, axis=0)

    def part_copy(dm, dt):
        n = dm * tiles + dt - 1
        return pltpu.make_async_remote_copy(
            src_ref=parts.at[tile, member],
            dst_ref=parts.at[tile, member],
            send_sem=part_send.at[n],
            recv_sem=part_recv.at[n],
            device_id=peer(dm, dt),
            device_id_type=MESH,
        )

    for_peers(lambda dm, dt: part_copy(dm, dt).start())
    for copy in obs_copies:
        copy.wait_recv()
    for_peers(lambda dm, dt: part_copy(dm, dt).wait_recv())

    @pl.when(has_lo)
    def _():
        for copy in downs:
            copy.wait_send()

    @pl.when(has_hi)
    def _():
        for copy in ups:
            copy.wait_send()

    for copy in obs_copies:
        copy.wait_send()
    for_peers(lambda dm, dt: part_copy(dm, dt).wait_send())


def finish(new_ref, parts, obs_all, new_hbm, rates_hbm, gram_hbm, rates, gram, out_sem):
    tile = lax.axis_index("tile")
    member = lax.axis_index("member")
    tiles, members = parts.shape[0:2]
    wells_dev = rates.shape[2]
    wells = wells_dev * tiles
    new_out = pltpu.make_async_copy(new_ref, new_hbm, out_sem.at[0])
    new_out.start()

    def tile_sum(m):
        whole = parts[0, m]
        for t in range(1, tiles):
            whole = whole + parts[t, m]
        return whole

    mine = tile_sum(member)
    for k in range(SUBSTEPS):
        row, lane = divmod(k * wells, LANES)
        moved = pltpu.roll(
            mine[row : row + 1], lax.rem(2 * LANES - lane - tile * wells_dev, LANES), 1
        )
        rates[k] = moved[:, 0:wells_dev]
    rates_out = pltpu.make_async_copy(rates, rates_hbm, out_sem.at[1])
    rates_out.start()
    obs = obs_all[0]
    for t in range(1, tiles):
        obs = obs * obs_all[t]
    data = [tile_sum(m) / obs for m in range(members)]
    mean = data[0]
    for m in range(1, members):
        mean = mean + data[m]
    mean = mean * (1.0 / members)
    own = mine / obs - mean
    terms = jnp.concatenate(
        [jnp.sum(own * (data[m] - mean), axis=0, keepdims=True) for m in range(members)], axis=0
    )
    terms = jnp.sum(terms, axis=1, keepdims=True)
    square = (members, LANES)
    diagonal = lax.broadcasted_iota(jnp.int32, square, 0) == lax.broadcasted_iota(
        jnp.int32, square, 1
    )
    line = jnp.sum(jnp.where(diagonal, terms, 0.0), axis=0, keepdims=True)
    gram[...] = line[:, 0:members] / (members - 1.0)
    gram_out = pltpu.make_async_copy(gram, gram_hbm, out_sem.at[2])
    gram_out.start()
    new_out.wait()
    rates_out.wait()
    gram_out.wait()


def body(tiles, members, sat, mob, pore, qx, qy, qz, cell, well, factor, obs):
    block = sat.shape[1:]
    rows, layers, columns = block
    conns = cell.shape[0]
    wells_dev = obs.shape[0]
    f32 = jnp.float32
    dma = pltpu.SemaphoreType.DMA
    hbm_spec = pl.BlockSpec(memory_space=pltpu.HBM)
    vmem_spec = pl.BlockSpec(memory_space=pltpu.VMEM)
    lines = -(-SUBSTEPS * wells_dev * tiles // LANES)
    new, parts, obs_all = pl.pallas_call(
        functools.partial(kernel, tiles, members),
        out_shape=(
            pltpu.VMEM(sat.shape, f32),
            pltpu.VMEM((tiles, members, lines, LANES), f32),
            pltpu.VMEM((tiles, lines, LANES), f32),
        ),
        in_specs=[hbm_spec] * 10,
        out_specs=(vmem_spec,) * 3,
        scratch_shapes=[pltpu.VMEM(block, f32)] * 6
        + [
            pltpu.VMEM((1, conns), jnp.int32),
            pltpu.VMEM((1, conns), jnp.int32),
            pltpu.VMEM((1, conns), f32),
            pltpu.VMEM((SUBSTEPS, wells_dev), f32),
            pltpu.VMEM((SUBSTEPS + 1,) + block, f32),
            pltpu.VMEM((2, layers, columns), f32),
            pltpu.VMEM((2, layers, columns), f32),
            pltpu.VMEM((2, layers, columns), f32),
            pltpu.VMEM((2, layers, columns), f32),
            pltpu.VMEM((2, 4, layers, columns), f32),
            pltpu.VMEM((layers, columns), f32),
            pltpu.VMEM((2, layers, columns), f32),
            pltpu.VMEM((4, layers, columns), f32),
            pltpu.VMEM((2, rows * layers, 2 * columns), jnp.bfloat16),
            pltpu.VMEM((conns, rows * layers), jnp.bfloat16),
            pltpu.VMEM((conns, LANES), f32),
            pltpu.VMEM((conns, LANES), f32),
            pltpu.VMEM((SUBLANES, LANES), f32),
            dma((14,)),
            dma((2, 8)),
            dma((2, 8)),
            dma((tiles - 1,)),
            dma((tiles - 1,)),
            dma((tiles * members - 1,)),
            dma((tiles * members - 1,)),
        ],
        compiler_params=pltpu.CompilerParams(
            collective_id=0, has_side_effects=True, vmem_limit_bytes=RUN_VMEM
        ),
        cost_estimate=pl.CostEstimate(
            flops=100 * SUBSTEPS * rows * layers * columns,
            bytes_accessed=28 * rows * layers * columns,
            transcendentals=0,
        ),
        name="transport",
    )(sat, mob, pore, qx, qy, qz, cell.reshape(1, -1), well.reshape(1, -1), factor.reshape(1, -1), obs.T)
    new, rates, gram = pl.pallas_call(
        finish,
        out_shape=(
            jax.ShapeDtypeStruct(sat.shape, f32),
            jax.ShapeDtypeStruct((SUBSTEPS, 1, wells_dev), f32),
            jax.ShapeDtypeStruct((1, members), f32),
        ),
        in_specs=[vmem_spec] * 3,
        out_specs=(hbm_spec,) * 3,
        scratch_shapes=[
            pltpu.VMEM((SUBSTEPS, 1, wells_dev), f32),
            pltpu.VMEM((1, members), f32),
            dma((3,)),
        ],
        compiler_params=pltpu.CompilerParams(vmem_limit_bytes=OUT_VMEM),
        name="finish",
    )(new, parts, obs_all)
    return new, jnp.transpose(rates, (1, 2, 0)), gram


def solution(mesh):
    field = P("member", "tile", None, None)
    in_specs = (field,) * 6 + (P("tile"), P("tile"), P("tile"), P("tile", None))
    out_specs = (field, P("member", "tile", None), P("member", None))
    run = functools.partial(body, mesh.shape["tile"], mesh.shape["member"])
    return jax.shard_map(run, mesh=mesh, in_specs=in_specs, out_specs=out_specs, check_vma=False)
```
